32 devices in a mesh: seq: 4 (over z), blk: 8 (over y, x, core).
Axes of the slice: x: 2, y: 2, z: 4, core: 2. Of those that a mesh axis runs over, the one named last changes fastest.
Arguments:
- train_acts: bfloat16 [4096, 4096], P(('seq', 'blk')), may hold values from -6 to 6
- train_grads: bfloat16 [4096, 14336], P(('seq', 'blk')), may hold values from -0.0234375 to 0.0234375
- block_table: int32 [8, 2], replicated, may hold values from 0 to 55, as said below
- seq_lengths: int32 [4], replicated, may hold values from 256 to 1024, as said below
- query_acts: bfloat16 [8, 256, 256], P('blk', 'seq'), may hold values from -6 to 6
- query_grads: bfloat16 [8, 256, 256], P('blk', 'seq'), may hold values from -6 to 6
- basis_acts: bfloat16 [8, 256, 256], P('blk', 'seq'), may hold values from -0.375 to 0.375
- basis_grads: bfloat16 [8, 256, 256], P('blk', 'seq'), may hold values from -0.375 to 0.375
- eigenvalues: float32 [8, 256, 256], P('blk', 'seq'), may hold values from 0.05 to 5
Outputs:
- scores: float32 [8, 4096], P(None, ('seq', 'blk'))
The draws below stay inside these ranges and needn't reach their ends.
Inputs may be any that keep to these rules, and one draw needn't show every extreme that they name: `block_table`: column 0 of a row is an output-gradient block below 56, column 1 an activation block below 16; the last gradient block is named by some row. `seq_lengths`: some sequence has all 1024 tokens and some other one a quarter of them.
All inputs are finite; a program needn't handle non-finite values.
Results may differ from the reference program's by a relative error of at most 0.02.
Values may be sent and summed in bfloat16 or wider, within the bound.
No kernel may reach another device: no remote copies, remote signals or barrier semaphores. Data moves between devices by JAX's collectives and lax.ppermute only.
A program may use at most 64 MiB of HBM per device.

```python
import math
import jax
import jax.numpy as jnp
from jax import lax

BLOCK = 256
D_WIN = 4096
FF_WIN = 14336
SEQ_LEN = 1024
QUERIES = 8
QTOK = 32
AB = 16
GB = 56
PAIRS = 8
TOKENS = 4096
SEQS = 4
QROWS = 256


def draw_block_table(key, part):
    first, second, third = jax.random.split(jax.random.fold_in(key, 11), 3)
    grad_index = jax.random.randint(first, (PAIRS,), 0, GB)
    act_index = jax.random.randint(second, (PAIRS,), 0, AB)
    chosen = jax.random.randint(third, (), 0, PAIRS)
    grad_index = jnp.where(jnp.arange(PAIRS) == chosen, GB - 1, grad_index)
    return jnp.stack([grad_index, act_index], axis=1).astype(jnp.int32)


def draw_seq_lengths(key, part):
    first, second, third = jax.random.split(jax.random.fold_in(key, 23), 3)
    lengths = jax.random.randint(first, (SEQS,), SEQ_LEN // 4, SEQ_LEN + 1)
    longest = jax.random.randint(second, (), 0, SEQS)
    shortest = (longest + 1 + jax.random.randint(third, (), 0, SEQS - 1)) % SEQS
    indices = jnp.arange(SEQS)
    lengths = jnp.where(indices == longest, SEQ_LEN, lengths)
    lengths = jnp.where(indices == shortest, SEQ_LEN // 4, lengths)
    return lengths.astype(jnp.int32)


def block_levels(own_key, shape, cuts, smallest, high):
    level = 1.0
    for dim, shards_of in cuts:
        draws = jax.random.uniform(jax.random.fold_in(jax.random.fold_in(own_key, 6), dim), (shards_of,), jnp.float32, smallest / len(cuts), high / len(cuts))
        level = level * jnp.repeat(jnp.exp(draws), shape[dim] // shards_of).reshape((-1,) + (1,) * (len(shape) - 1 - dim))
    return level


def noise(key, shape, scale, limit, cuts=(), kind=jnp.bfloat16):
    result = jax.random.normal(key, shape, jnp.float32) * scale
    if len(cuts) > 0:
        result = block_levels(key, shape, cuts, -0.22, 0.18) * result
    return jnp.clip(result, min=-limit, max=limit).astype(kind)


def setup_inputs(seed: int = 0) -> dict:
    key_of = jax.random.split(jax.random.key(seed), 10)
    return {
        "train_acts": noise(key_of[0], (TOKENS, D_WIN), 1.0, 6.0, ((0, 32),)),
        "train_grads": noise(key_of[1], (TOKENS, FF_WIN), (BLOCK * BLOCK) ** -0.5, 0.0234375, ((0, 32),)),
        "block_table": draw_block_table(jax.random.fold_in(key_of[9], 71), 0),
        "seq_lengths": draw_seq_lengths(jax.random.fold_in(key_of[9], 71), 0),
        "query_acts": noise(key_of[4], (PAIRS, QROWS, BLOCK), 1.0, 6.0, ((0, 8), (1, 4))),
        "query_grads": noise(key_of[5], (PAIRS, QROWS, BLOCK), 1.0, 6.0, ((0, 8), (1, 4))),
        "basis_acts": noise(key_of[6], (PAIRS, BLOCK, BLOCK), BLOCK ** -0.5, 0.375, ((0, 8), (1, 4))),
        "basis_grads": noise(key_of[7], (PAIRS, BLOCK, BLOCK), BLOCK ** -0.5, 0.375, ((0, 8), (1, 4))),
        "eigenvalues": jnp.clip(jnp.exp(math.log(5.0) - 4.6051702 * jax.random.uniform(key_of[8], (PAIRS, BLOCK, BLOCK), jnp.float32) ** block_levels(key_of[8], (PAIRS, BLOCK, BLOCK), ((0, 8), (1, 4)), -0.2, 0.2)), 0.05, 5.0),
    }


DAMPING = 0.1


def reference(train_acts, train_grads, block_table, seq_lengths, query_acts, query_grads, basis_acts, basis_grads, eigenvalues):
    act_blocks = train_acts.reshape(TOKENS, AB, BLOCK)
    grad_blocks = train_grads.reshape(TOKENS, GB, BLOCK)
    block_rows = math.gcd(TOKENS, 512)

    def one_pair(running, owner):
        grad_index = block_table[owner, 0]
        act_index = block_table[owner, 1]
        act_sel = jnp.take(act_blocks, act_index, axis=1)
        grad_sel = jnp.take(grad_blocks, grad_index, axis=1)
        rot_acts = jnp.dot(act_sel, basis_acts[owner], preferred_element_type=jnp.float32).astype(jnp.bfloat16)
        rot_grads = jnp.dot(grad_sel, basis_grads[owner], preferred_element_type=jnp.float32).astype(jnp.bfloat16)
        qrot_acts = jnp.dot(query_acts[owner], basis_acts[owner], preferred_element_type=jnp.float32).astype(jnp.bfloat16)
        qrot_grads = jnp.dot(query_grads[owner], basis_grads[owner], preferred_element_type=jnp.float32).astype(jnp.bfloat16)
        qrot_acts = qrot_acts.reshape(QUERIES, QTOK, BLOCK).astype(jnp.float32)
        qrot_grads = qrot_grads.reshape(QUERIES, QTOK, BLOCK).astype(jnp.float32)
        outer = jnp.einsum("qsi,qsj->qij", qrot_grads, qrot_acts)
        precond = (outer / QTOK / (eigenvalues[owner] + DAMPING)[None, :, :]).astype(jnp.bfloat16)
        right_mat = jnp.transpose(precond, (2, 0, 1)).reshape(BLOCK, QUERIES * BLOCK)

        def block_scores(pieces):
            act_piece, grad_piece = pieces
            mixed = jnp.dot(act_piece, right_mat, preferred_element_type=jnp.float32).reshape(-1, QUERIES, BLOCK)
            return jnp.sum(mixed * grad_piece.astype(jnp.float32)[:, None, :], axis=2)

        partial_value = lax.map(block_scores, (rot_acts.reshape(-1, block_rows, BLOCK), rot_grads.reshape(-1, block_rows, BLOCK)))
        return running + partial_value.reshape(TOKENS, QUERIES), None

    total, _ = lax.scan(one_pair, jnp.zeros((TOKENS, QUERIES), jnp.float32), jnp.arange(PAIRS, dtype=jnp.int32))
    position = jnp.arange(TOKENS, dtype=jnp.int32)
    valid = (position % SEQ_LEN) < seq_lengths[position // SEQ_LEN]
    return jnp.where(valid[None, :], total.T, jnp.zeros((), jnp.float32))
```

```python
import functools

import jax
import jax.numpy as jnp
from jax import lax
from jax.experimental import pallas as pl
from jax.experimental.pallas import tpu as pltpu
from jax.sharding import PartitionSpec as P

BLOCK = 256
SEQ_LEN = 1024
QUERIES = 8
QTOK = 32
DAMPING = 0.1
VMEM_BYTES = 24 * 1024 * 1024

VMEM = pl.BlockSpec(memory_space=pltpu.VMEM)
SMEM = pl.BlockSpec(memory_space=pltpu.SMEM)
ANY = pl.BlockSpec(memory_space=pl.ANY)
NT = (((1,), (1,)), ((), ()))
TN = (((0,), (0,)), ((), ()))


def select_kernel(table_ref, acts_ref, grads_ref, out_ref, sem):
    pairs = out_ref.shape[0]
    copies = []
    for k in range(pairs):
        for half, (src, column) in enumerate(((acts_ref, 1), (grads_ref, 0))):
            start = pl.multiple_of(table_ref[k, column] * BLOCK, BLOCK)
            copy = pltpu.make_async_copy(
                src.at[:, pl.ds(start, BLOCK)],
                out_ref.at[k, :, pl.ds(half * BLOCK, BLOCK)],
                sem.at[2 * k + half],
            )
            copy.start()
            copies.append(copy)
    for copy in copies:
        copy.wait()


def select_blocks(table, acts, grads):
    pairs, tokens = table.shape[0], acts.shape[0]
    return pl.pallas_call(
        select_kernel,
        out_shape=jax.ShapeDtypeStruct((pairs, tokens, 2 * BLOCK), jnp.bfloat16),
        in_specs=[SMEM, ANY, ANY],
        out_specs=ANY,
        scratch_shapes=[pltpu.SemaphoreType.DMA((2 * pairs,))],
        compiler_params=pltpu.CompilerParams(vmem_limit_bytes=VMEM_BYTES),
        cost_estimate=pl.CostEstimate(
            flops=0, bytes_accessed=pairs * tokens * BLOCK * 8, transcendentals=0
        ),
        name="select_blocks",
    )(table, acts, grads)


def precond_kernel(shifts, rows, *refs):
    pieces = refs[:shifts]
    basis_act_ref, basis_grad_t_ref, precond_ref, full = refs[shifts:]
    me = lax.axis_index("seq")
    for m, piece in enumerate(pieces):
        owner = lax.rem(me - m + shifts, shifts)
        place = pl.ds(pl.multiple_of(owner * rows, rows), rows)
        for part in range(5):
            full[part, place, :] = piece[part * rows : (part + 1) * rows, :]
    basis_act, basis_grad = full[0], full[1]
    basis_act_ref[...] = basis_act
    basis_grad_t_ref[...] = basis_grad.astype(jnp.float32).T.astype(jnp.bfloat16)
    qrot_acts = jnp.dot(full[2], basis_act, preferred_element_type=jnp.float32).astype(jnp.bfloat16)
    qrot_grads = jnp.dot(full[3], basis_grad, preferred_element_type=jnp.float32).astype(jnp.bfloat16)
    scale = 1.0 / (QTOK * (full[4].astype(jnp.float32) + DAMPING))
    for q in range(QUERIES):
        tokens = slice(q * QTOK, (q + 1) * QTOK)
        outer = lax.dot_general(
            qrot_grads[tokens], qrot_acts[tokens], TN, preferred_element_type=jnp.float32
        )
        precond_ref[q] = (outer * scale).astype(jnp.bfloat16)


def make_precond(pieces):
    shifts, rows = len(pieces), pieces[0].shape[0] // 5
    square = jax.ShapeDtypeStruct((BLOCK, BLOCK), jnp.bfloat16)
    return pl.pallas_call(
        functools.partial(precond_kernel, shifts, rows),
        out_shape=(square, square, jax.ShapeDtypeStruct((QUERIES, BLOCK, BLOCK), jnp.bfloat16)),
        in_specs=[VMEM] * shifts,
        out_specs=(VMEM, VMEM, VMEM),
        scratch_shapes=[pltpu.VMEM((5, BLOCK, BLOCK), jnp.bfloat16)],
        compiler_params=pltpu.CompilerParams(vmem_limit_bytes=VMEM_BYTES),
        cost_estimate=pl.CostEstimate(
            flops=2 * BLOCK**3 * 3, bytes_accessed=2 * BLOCK * BLOCK * 15, transcendentals=0
        ),
        name="make_precond",
    )(*pieces)


def score_kernel(lengths_ref, slices_ref, basis_act_ref, basis_grad_t_ref, precond_ref, out_ref):
    sources, tokens = slices_ref.shape[0], slices_ref.shape[1]
    first = lax.axis_index("seq") * sources * tokens
    step = 2 if sources % 2 == 0 else 1

    def chunk(c, carry):
        acts = slices_ref[pl.ds(c * step, step), :, :BLOCK].reshape(step * tokens, BLOCK)
        grads = slices_ref[pl.ds(c * step, step), :, BLOCK:].reshape(step * tokens, BLOCK)
        rot_acts = jnp.dot(acts, basis_act_ref[...], preferred_element_type=jnp.float32).astype(
            jnp.bfloat16
        )
        rot_grads = lax.dot_general(
            basis_grad_t_ref[...], grads, NT, preferred_element_type=jnp.float32
        )
        rows = []
        for q in range(QUERIES):
            mixed = lax.dot_general(
                precond_ref[q], rot_acts, NT, preferred_element_type=jnp.float32
            )
            rows.append(jnp.sum(mixed * rot_grads, axis=0, keepdims=True))
        scores = jnp.concatenate(rows, axis=0)
        start = first + c * step * tokens
        position = start + lax.broadcasted_iota(jnp.int32, scores.shape, 1)
        low = start // SEQ_LEN
        valid = jnp.zeros(scores.shape, jnp.bool_)
        for s in range((step * tokens + SEQ_LEN - 2) // SEQ_LEN + 1):
            sequence = jnp.minimum(low + s, lengths_ref.shape[0] - 1)
            offset = position - sequence * SEQ_LEN
            valid |= (offset >= 0) & (offset < lengths_ref[sequence])
        scores = jnp.where(valid, scores, 0.0)
        for s in range(step):
            out_ref[c * step + s] = scores[:, s * tokens : (s + 1) * tokens]
        return carry

    lax.fori_loop(0, sources // step, chunk, 0, unroll=True if sources <= 8 else 1)


def partial_scores(lengths, slices, basis_act, basis_grad_t, precond):
    sources, tokens, _ = slices.shape
    return pl.pallas_call(
        score_kernel,
        out_shape=jax.ShapeDtypeStruct((sources, QUERIES, tokens), jnp.float32),
        in_specs=[SMEM, VMEM, VMEM, VMEM, VMEM],
        out_specs=VMEM,
        compiler_params=pltpu.CompilerParams(vmem_limit_bytes=VMEM_BYTES),
        cost_estimate=pl.CostEstimate(
            flops=2 * sources * tokens * BLOCK * BLOCK * (QUERIES + 2),
            bytes_accessed=slices.size * 2 + precond.size * 2,
            transcendentals=0,
        ),
        name="partial_scores",
    )(lengths, slices, basis_act, basis_grad_t, precond)


def on_device(
    train_acts,
    train_grads,
    block_table,
    seq_lengths,
    query_acts,
    query_grads,
    basis_acts,
    basis_grads,
    eigenvalues,
):
    groups = lax.axis_size("seq")
    packed = jnp.concatenate(
        [
            basis_acts[0],
            basis_grads[0],
            query_acts[0],
            query_grads[0],
            eigenvalues[0].astype(jnp.bfloat16),
        ],
        axis=0,
    )
    pieces = [packed]
    for m in range(1, groups):
        pieces.append(lax.ppermute(packed, "seq", [(i, (i + m) % groups) for i in range(groups)]))
    slices = select_blocks(block_table, train_acts, train_grads)
    received = lax.all_to_all(slices, "blk", split_axis=0, concat_axis=0, tiled=True)
    basis_act, basis_grad_t, precond = make_precond(pieces)
    partial = partial_scores(seq_lengths, received, basis_act, basis_grad_t, precond)
    spread = lax.all_to_all(partial, "blk", split_axis=0, concat_axis=0, tiled=True)
    return jnp.sum(spread, axis=0)


def solution(mesh):
    in_specs = (
        P(("seq", "blk"), None),
        P(("seq", "blk"), None),
        P(),
        P(),
        P("blk", "seq", None),
        P("blk", "seq", None),
        P("blk", "seq", None),
        P("blk", "seq", None),
        P("blk", "seq", None),
    )
    out_specs = P(None, ("seq", "blk"))
    return jax.shard_map(
        on_device, mesh=mesh, in_specs=in_specs, out_specs=out_specs, check_vma=False
    )
```

```python
import functools

import jax
import jax.numpy as jnp
from jax import lax
from jax.experimental import pallas as pl
from jax.experimental.pallas import tpu as pltpu
from jax.sharding import PartitionSpec as P

BLOCK = 256
SEQ_LEN = 1024
QUERIES = 8
QTOK = 32
DAMPING = 0.1
CORES = 2
PACK_VMEM = 16 * 1024 * 1024
VMEM_BYTES = 24 * 1024 * 1024

VMEM = pl.BlockSpec(memory_space=pltpu.VMEM)
SMEM = pl.BlockSpec(memory_space=pltpu.SMEM)
HBM = pl.BlockSpec(memory_space=pltpu.HBM)
NT = (((1,), (1,)), ((), ()))
TN = (((0,), (0,)), ((), ()))


def swap(array, axis, bits):
    return lax.ppermute(array, axis, [(i, i ^ bits) for i in range(lax.axis_size(axis))])


def pack_kernel(table_ref, acts_ref, grads_ref, *refs):
    shards, packed_ref = refs[:5], refs[5]
    chunks, raw_eigen, sem = refs[6:-2], refs[-2], refs[-1]
    me = lax.axis_index("blk")
    rows = raw_eigen.shape[0]
    copies = []
    for part, shard in enumerate(shards):
        target = raw_eigen if part == 4 else packed_ref.at[pl.ds(part * rows, rows), :]
        copies.append(pltpu.make_async_copy(shard.at[0], target, sem.at[part]))
    for m, chunk in enumerate(chunks):
        for core in range(CORES):
            owner = me ^ (CORES * m + core)
            for half, (source, row) in enumerate(((acts_ref, 1), (grads_ref, 0))):
                start = pl.multiple_of(table_ref[row, owner] * BLOCK, BLOCK)
                copies.append(
                    pltpu.make_async_copy(
                        source.at[:, pl.ds(start, BLOCK)],
                        chunk.at[core, :, pl.ds(half * BLOCK, BLOCK)],
                        sem.at[len(copies)],
                    )
                )
    for copy in copies:
        copy.start()
    for copy in copies[:5]:
        copy.wait()
    packed_ref[4 * rows :, :] = raw_eigen[...].astype(jnp.bfloat16)
    for copy in copies[5:]:
        copy.wait()


def pack(table, acts, grads, *shards):
    pairs, tokens, rows = table.shape[1], acts.shape[0], shards[0].shape[1]
    chunk = pltpu.VMEM((CORES, tokens, 2 * BLOCK), jnp.bfloat16)
    packed = pltpu.VMEM((5 * rows, BLOCK), jnp.bfloat16)
    large = [pltpu.with_memory_space_constraint(a, pltpu.HBM) for a in (acts, grads, *shards)]
    chips = pairs // CORES
    return pl.pallas_call(
        pack_kernel,
        out_shape=(packed,) + (chunk,) * chips,
        in_specs=[SMEM] + [HBM] * 7,
        out_specs=(VMEM,) * (1 + chips),
        scratch_shapes=[
            pltpu.VMEM((rows, BLOCK), jnp.float32),
            pltpu.SemaphoreType.DMA((5 + 2 * pairs,)),
        ],
        compiler_params=pltpu.CompilerParams(vmem_limit_bytes=PACK_VMEM),
        cost_estimate=pl.CostEstimate(
            flops=0, bytes_accessed=pairs * tokens * BLOCK * 8, transcendentals=0
        ),
        name="pack",
    )(table, *large)


def precond_kernel(rows, *refs):
    pieces = refs[:-4]
    basis_act_ref, basis_grad_t_ref, precond_ref, full = refs[-4:]
    me = lax.axis_index("seq")
    for m, piece in enumerate(pieces):
        place = pl.ds(pl.multiple_of((me ^ m) * rows, rows), rows)
        for part in range(5):
            full[part, place, :] = piece[part * rows : (part + 1) * rows, :]
    basis_act, basis_grad = full[0], full[1]
    basis_act_ref[...] = basis_act
    basis_grad_t_ref[...] = basis_grad.astype(jnp.float32).T.astype(jnp.bfloat16)
    qrot_acts = jnp.dot(full[2], basis_act, preferred_element_type=jnp.float32).astype(jnp.bfloat16)
    qrot_grads = jnp.dot(full[3], basis_grad, preferred_element_type=jnp.float32).astype(jnp.bfloat16)
    scale = 1.0 / (QTOK * (full[4].astype(jnp.float32) + DAMPING))
    for q in range(QUERIES):
        tokens = slice(q * QTOK, (q + 1) * QTOK)
        outer = lax.dot_general(
            qrot_grads[tokens], qrot_acts[tokens], TN, preferred_element_type=jnp.float32
        )
        precond_ref[q] = (outer * scale).astype(jnp.bfloat16)


def make_precond(pieces):
    rows = pieces[0].shape[0] // 5
    square = jax.ShapeDtypeStruct((BLOCK, BLOCK), jnp.bfloat16)
    return pl.pallas_call(
        functools.partial(precond_kernel, rows),
        out_shape=(square, square, jax.ShapeDtypeStruct((QUERIES, BLOCK, BLOCK), jnp.bfloat16)),
        in_specs=[VMEM] * len(pieces),
        out_specs=(VMEM, VMEM, VMEM),
        scratch_shapes=[pltpu.VMEM((5, BLOCK, BLOCK), jnp.bfloat16)],
        compiler_params=pltpu.CompilerParams(vmem_limit_bytes=VMEM_BYTES),
        cost_estimate=pl.CostEstimate(
            flops=2 * BLOCK**3 * 3, bytes_accessed=2 * BLOCK * BLOCK * 15, transcendentals=0
        ),
        name="make_precond",
    )(*pieces)


def valid_mask(lengths_ref, start, shape):
    position = start + lax.broadcasted_iota(jnp.int32, shape, 1)
    low = start // SEQ_LEN
    valid = jnp.zeros(shape, jnp.bool_)
    for s in range((shape[1] + SEQ_LEN - 2) // SEQ_LEN + 1):
        sequence = jnp.minimum(low + s, lengths_ref.shape[0] - 1)
        offset = position - sequence * SEQ_LEN
        valid |= (offset >= 0) & (offset < lengths_ref[sequence])
    return valid


def score_kernel(core, chips, lengths_ref, basis_act_ref, basis_grad_t_ref, precond_ref, *refs):
    chunks, before, outs = refs[:chips], refs[chips : -chips], refs[-chips:]
    tokens = chunks[0].shape[1]
    me = lax.axis_index("blk")
    group = lax.axis_index("seq") * lax.axis_size("blk")
    for m in range(0, chips, 2):
        both = chunks[m : m + 2]
        acts = jnp.concatenate([c[core, :, :BLOCK] for c in both], axis=0)
        grads = jnp.concatenate([c[core, :, BLOCK:] for c in both], axis=0)
        rot_acts = jnp.dot(acts, basis_act_ref[...], preferred_element_type=jnp.float32).astype(
            jnp.bfloat16
        )
        rot_grads = lax.dot_general(
            basis_grad_t_ref[...], grads, NT, preferred_element_type=jnp.float32
        )
        rows = []
        for q in range(QUERIES):
            mixed = lax.dot_general(
                precond_ref[q], rot_acts, NT, preferred_element_type=jnp.float32
            )
            rows.append(jnp.sum(mixed * rot_grads, axis=0, keepdims=True))
        scores = jnp.concatenate(rows, axis=0)
        for s in range(len(both)):
            part = scores[:, s * tokens : (s + 1) * tokens]
            if core:
                start = (group + (me ^ (CORES * (m + s)))) * tokens
                valid = valid_mask(lengths_ref, start, part.shape)
                part = jnp.where(valid, part + before[m + s][...], 0.0)
            outs[m + s][...] = part


def partial_scores(core, lengths, weights, chunks, before):
    chips, tokens = len(chunks), chunks[0].shape[1]
    return pl.pallas_call(
        functools.partial(score_kernel, core, chips),
        out_shape=(jax.ShapeDtypeStruct((QUERIES, tokens), jnp.float32),) * chips,
        in_specs=[SMEM] + [VMEM] * (3 + chips + len(before)),
        out_specs=(VMEM,) * chips,
        compiler_params=pltpu.CompilerParams(vmem_limit_bytes=VMEM_BYTES),
        cost_estimate=pl.CostEstimate(
            flops=2 * chips * tokens * BLOCK * BLOCK * (QUERIES + 2),
            bytes_accessed=2 * BLOCK * (chips * tokens * 2 + BLOCK * (QUERIES + 2)),
            transcendentals=0,
        ),
        name="partial_scores",
    )(lengths, *weights, *chunks, *before)


def on_device(
    train_acts,
    train_grads,
    block_table,
    seq_lengths,
    query_acts,
    query_grads,
    basis_acts,
    basis_grads,
    eigenvalues,
):
    groups, chips = lax.axis_size("seq"), lax.axis_size("blk") // CORES
    packed, *chunks = pack(
        block_table.T,
        train_acts,
        train_grads,
        basis_acts,
        basis_grads,
        query_acts,
        query_grads,
        eigenvalues,
    )
    own = [packed] + [swap(packed, "seq", m) for m in range(1, groups)]
    chunks = chunks[:1] + [swap(chunks[m], "blk", CORES * m) for m in range(1, chips)]
    other = [swap(piece, "blk", 1) for piece in own]
    scores = partial_scores(0, seq_lengths, make_precond(own), chunks, ())
    scores = partial_scores(1, seq_lengths, make_precond(other), chunks, scores)
    total = scores[0]
    for m in range(1, chips):
        total = total + swap(scores[m], "blk", CORES * m)
    return total


def solution(mesh):
    in_specs = (
        P(("seq", "blk"), None),
        P(("seq", "blk"), None),
        P(),
        P(),
        P("blk", "seq", None),
        P("blk", "seq", None),
        P("blk", "seq", None),
        P("blk", "seq", None),
        P("blk", "seq", None),
    )
    out_specs = P(None, ("seq", "blk"))
    return jax.shard_map(
        on_device, mesh=mesh, in_specs=in_specs, out_specs=out_specs, check_vma=False
    )
```

```python
import functools

import jax
import jax.numpy as jnp
from jax import lax
from jax.experimental import pallas as pl
from jax.experimental.pallas import tpu as pltpu
from jax.sharding import PartitionSpec as P

BLOCK = 256
SEQ_LEN = 1024
QUERIES = 8
QTOK = 32
DAMPING = 0.1
CORES = 2
PACK_VMEM = 16 * 1024 * 1024
VMEM_BYTES = 24 * 1024 * 1024

VMEM = pl.BlockSpec(memory_space=pltpu.VMEM)
SMEM = pl.BlockSpec(memory_space=pltpu.SMEM)
HBM = pl.BlockSpec(memory_space=pltpu.HBM)
NT = (((1,), (1,)), ((), ()))
TN = (((0,), (0,)), ((), ()))


def swap(array, axis, bits):
    return lax.ppermute(array, axis, [(i, i ^ bits) for i in range(lax.axis_size(axis))])


def pack_kernel(table_ref, acts_ref, grads_ref, *refs):
    shards, packed_ref = refs[:5], refs[5]
    chunks, raw_eigen, sem = refs[6:-2], refs[-2], refs[-1]
    me = lax.axis_index("blk")
    rows = raw_eigen.shape[0]
    copies = []
    for part, shard in enumerate(shards):
        target = raw_eigen if part == 4 else packed_ref.at[pl.ds(part * rows, rows), :]
        copies.append(pltpu.make_async_copy(shard.at[0], target, sem.at[part]))
    for m, chunk in enumerate(chunks):
        for core in range(CORES):
            owner = me ^ (CORES * m + core)
            for half, (source, row) in enumerate(((acts_ref, 1), (grads_ref, 0))):
                start = pl.multiple_of(table_ref[row, owner] * BLOCK, BLOCK)
                copies.append(
                    pltpu.make_async_copy(
                        source.at[:, pl.ds(start, BLOCK)],
                        chunk.at[core, :, pl.ds(half * BLOCK, BLOCK)],
                        sem.at[len(copies)],
                    )
                )
    for copy in copies:
        copy.start()
    for copy in copies[:5]:
        copy.wait()
    packed_ref[4 * rows :, :] = raw_eigen[...].astype(jnp.bfloat16)
    for copy in copies[5:]:
        copy.wait()


def pack(table, acts, grads, *shards):
    pairs, tokens, rows = table.shape[1], acts.shape[0], shards[0].shape[1]
    chunk = pltpu.VMEM((CORES, tokens, 2 * BLOCK), jnp.bfloat16)
    packed = pltpu.VMEM((5 * rows, BLOCK), jnp.bfloat16)
    table, *large = [pltpu.with_memory_space_constraint(a, pltpu.HBM) for a in (table, acts, grads, *shards)]
    chips = pairs // CORES
    return pl.pallas_call(
        pack_kernel,
        out_shape=(packed,) + (chunk,) * chips,
        in_specs=[SMEM] + [HBM] * 7,
        out_specs=(VMEM,) * (1 + chips),
        scratch_shapes=[
            pltpu.VMEM((rows, BLOCK), jnp.float32),
            pltpu.SemaphoreType.DMA((5 + 2 * pairs,)),
        ],
        compiler_params=pltpu.CompilerParams(vmem_limit_bytes=PACK_VMEM),
        cost_estimate=pl.CostEstimate(
            flops=0, bytes_accessed=pairs * tokens * BLOCK * 8, transcendentals=0
        ),
        name="pack",
    )(table, *large)


def precond(full, basis_act_ref, basis_grad_t_ref, precond_ref):
    basis_act, basis_grad = full[0], full[1]
    basis_act_ref[...] = basis_act
    basis_grad_t_ref[...] = basis_grad.astype(jnp.float32).T.astype(jnp.bfloat16)
    qrot_acts = jnp.dot(full[2], basis_act, preferred_element_type=jnp.float32).astype(jnp.bfloat16)
    qrot_grads = jnp.dot(full[3], basis_grad, preferred_element_type=jnp.float32).astype(jnp.bfloat16)
    scale = 1.0 / (QTOK * (full[4].astype(jnp.float32) + DAMPING))
    for q in range(QUERIES):
        tokens = slice(q * QTOK, (q + 1) * QTOK)
        outer = lax.dot_general(
            qrot_grads[tokens], qrot_acts[tokens], TN, preferred_element_type=jnp.float32
        )
        precond_ref[q] = (outer * scale).astype(jnp.bfloat16)


def own_kernel(rows, *refs):
    pieces, full, weights = refs[:-4], refs[-4], refs[-3:]
    me = lax.axis_index("seq")
    for m, piece in enumerate(pieces):
        place = pl.ds(pl.multiple_of((me ^ m) * rows, rows), rows)
        for part in range(5):
            full[part, place, :] = piece[part * rows : (part + 1) * rows, :]
    precond(full, *weights)


def make_precond(kernel, name, operands, more):
    square = jax.ShapeDtypeStruct((BLOCK, BLOCK), jnp.bfloat16)
    outs = more + (square, square, jax.ShapeDtypeStruct((QUERIES, BLOCK, BLOCK), jnp.bfloat16))
    return pl.pallas_call(
        kernel,
        out_shape=outs,
        in_specs=[VMEM] * len(operands),
        out_specs=(VMEM,) * len(outs),
        compiler_params=pltpu.CompilerParams(vmem_limit_bytes=VMEM_BYTES),
        cost_estimate=pl.CostEstimate(
            flops=2 * BLOCK**3 * 3, bytes_accessed=2 * BLOCK * BLOCK * 15, transcendentals=0
        ),
        name=name,
    )(*operands)


def own_precond(pieces):
    rows = pieces[0].shape[0] // 5
    full = jax.ShapeDtypeStruct((5, BLOCK, BLOCK), jnp.bfloat16)
    return make_precond(functools.partial(own_kernel, rows), "own_precond", pieces, (full,))


def other_precond(full):
    return make_precond(precond, "other_precond", (full,), ())


def valid_mask(lengths_ref, start, shape):
    position = start + lax.broadcasted_iota(jnp.int32, shape, 1)
    low = start // SEQ_LEN
    valid = jnp.zeros(shape, jnp.bool_)
    for s in range((shape[1] + SEQ_LEN - 2) // SEQ_LEN + 1):
        sequence = jnp.minimum(low + s, lengths_ref.shape[0] - 1)
        offset = position - sequence * SEQ_LEN
        valid |= (offset >= 0) & (offset < lengths_ref[sequence])
    return valid


def score_kernel(core, chips, lengths_ref, basis_act_ref, basis_grad_t_ref, precond_ref, *refs):
    chunks, before, outs = refs[:chips], refs[chips : -chips], refs[-chips:]
    tokens = chunks[0].shape[1]
    me = lax.axis_index("blk")
    group = lax.axis_index("seq") * lax.axis_size("blk")
    for m in range(0, chips, 2):
        both = chunks[m : m + 2]
        acts = jnp.concatenate([c[core, :, :BLOCK] for c in both], axis=0)
        grads = jnp.concatenate([c[core, :, BLOCK:] for c in both], axis=0)
        rot_acts = jnp.dot(acts, basis_act_ref[...], preferred_element_type=jnp.float32).astype(
            jnp.bfloat16
        )
        rot_grads = lax.dot_general(
            basis_grad_t_ref[...], grads, NT, preferred_element_type=jnp.float32
        )
        rows = []
        for q in range(QUERIES):
            mixed = lax.dot_general(
                precond_ref[q], rot_acts, NT, preferred_element_type=jnp.float32
            )
            rows.append(jnp.sum(mixed * rot_grads, axis=0, keepdims=True))
        scores = jnp.concatenate(rows, axis=0)
        for s in range(len(both)):
            part = scores[:, s * tokens : (s + 1) * tokens]
            if core:
                start = (group + (me ^ (CORES * (m + s)))) * tokens
                valid = valid_mask(lengths_ref, start, part.shape)
                part = jnp.where(valid, part + before[m + s][...], 0.0)
            outs[m + s][...] = part


def partial_scores(core, lengths, weights, chunks, before):
    chips, tokens = len(chunks), chunks[0].shape[1]
    return pl.pallas_call(
        functools.partial(score_kernel, core, chips),
        out_shape=(jax.ShapeDtypeStruct((QUERIES, tokens), jnp.float32),) * chips,
        in_specs=[SMEM] + [VMEM] * (3 + chips + len(before)),
        out_specs=(VMEM,) * chips,
        compiler_params=pltpu.CompilerParams(vmem_limit_bytes=VMEM_BYTES),
        cost_estimate=pl.CostEstimate(
            flops=2 * chips * tokens * BLOCK * BLOCK * (QUERIES + 2),
            bytes_accessed=2 * BLOCK * (chips * tokens * 2 + BLOCK * (QUERIES + 2)),
            transcendentals=0,
        ),
        name="partial_scores",
    )(lengths, *weights, *chunks, *before)


def on_device(
    train_acts,
    train_grads,
    block_table,
    seq_lengths,
    query_acts,
    query_grads,
    basis_acts,
    basis_grads,
    eigenvalues,
):
    groups, chips = lax.axis_size("seq"), lax.axis_size("blk") // CORES
    packed, *chunks = pack(
        block_table.T,
        train_acts,
        train_grads,
        basis_acts,
        basis_grads,
        query_acts,
        query_grads,
        eigenvalues,
    )
    own = [packed]
    for m in range(1, groups):
        own.append(swap(own[m & (m - 1)], "seq", m & -m))
    chunks = chunks[:1] + [swap(chunks[m], "blk", CORES * m) for m in range(1, chips)]
    own, chunks = lax.optimization_barrier((own, chunks))
    full, *weights = own_precond(own)
    other = other_precond(swap(full, "blk", 1))
    scores = partial_scores(0, seq_lengths, weights, chunks, ())
    scores = partial_scores(1, seq_lengths, other, chunks, scores)
    total = scores[0]
    for m in range(1, chips):
        total = total + swap(scores[m], "blk", CORES * m)
    return total


def solution(mesh):
    in_specs = (
        P(("seq", "blk"), None),
        P(("seq", "blk"), None),
        P(),
        P(),
        P("blk", "seq", None),
        P("blk", "seq", None),
        P("blk", "seq", None),
        P("blk", "seq", None),
        P("blk", "seq", None),
    )
    out_specs = P(None, ("seq", "blk"))
    return jax.shard_map(
        on_device, mesh=mesh, in_specs=in_specs, out_specs=out_specs, check_vma=False
    )
```

```python
import functools

import jax
import jax.numpy as jnp
from jax import lax
from jax.experimental import pallas as pl
from jax.experimental.pallas import tpu as pltpu
from jax.sharding import PartitionSpec as P

BLOCK = 256
SEQ_LEN = 1024
QUERIES = 8
QTOK = 32
DAMPING = 0.1
CORES = 2
WIDTH = 4
PACK_VMEM = 16 * 1024 * 1024
VMEM_BYTES = 24 * 1024 * 1024

VMEM = pl.BlockSpec(memory_space=pltpu.VMEM)
HBM = pl.BlockSpec(memory_space=pltpu.HBM)
TT = (((0,), (1,)), ((), ()))
TN = (((0,), (0,)), ((), ()))


def swap(array, axis, bits):
    return lax.ppermute(array, axis, [(i, i ^ bits) for i in range(lax.axis_size(axis))])


def valid_mask(lengths, sequences, start, shape):
    position = start + lax.broadcasted_iota(jnp.int32, shape, 1)
    low = start // SEQ_LEN
    valid = jnp.zeros(shape, jnp.float32)
    for s in range((shape[1] + SEQ_LEN - 2) // SEQ_LEN + 1):
        sequence = jnp.minimum(low + s, sequences - 1)
        offset = position - sequence * SEQ_LEN
        valid = jnp.where((offset >= 0) & (offset < lengths[sequence]), 1.0, valid)
    return valid


def pack_kernel(table_ref, lengths_ref, acts_ref, grads_ref, *refs):
    shards, packed_ref, mask_ref = refs[:5], refs[5], refs[6]
    chunks, (raw_eigen, table, lengths, sem) = refs[7:-4], refs[-4:]
    me = lax.axis_index("blk")
    rows, tokens = raw_eigen.shape[0], acts_ref.shape[0]
    scalars = [
        pltpu.make_async_copy(table_ref, table, sem.at[0]),
        pltpu.make_async_copy(lengths_ref, lengths, sem.at[1]),
    ]
    weights = []
    for part, shard in enumerate(shards):
        target = raw_eigen if part == 4 else packed_ref.at[pl.ds(part * rows, rows), :]
        weights.append(pltpu.make_async_copy(shard.at[0], target, sem.at[2 + part]))
    for copy in scalars + weights:
        copy.start()
    scalars[0].wait()
    copies = []
    for m, chunk in enumerate(chunks):
        for core in range(CORES):
            owner = me ^ (CORES * m + core)
            for half, (source, row) in enumerate(((acts_ref, 1), (grads_ref, 0))):
                start = pl.multiple_of(table[row, owner] * BLOCK, BLOCK)
                copy = pltpu.make_async_copy(
                    source.at[:, pl.ds(start, BLOCK)],
                    chunk.at[core, :, pl.ds(half * BLOCK, BLOCK)],
                    sem.at[7 + len(copies)],
                )
                copy.start()
                copies.append(copy)
    scalars[1].wait()
    group = lax.axis_index("seq") * lax.axis_size("blk")
    for m in range(len(chunks)):
        start = (group + (me ^ (CORES * m))) * tokens
        mask_ref[m] = valid_mask(lengths, lengths_ref.shape[0], start, mask_ref.shape[1:])
    for copy in weights:
        copy.wait()
    packed_ref[4 * rows :, :] = raw_eigen[...].astype(jnp.bfloat16)
    for copy in copies:
        copy.wait()


def pack(table, lengths, acts, grads, *shards):
    pairs, tokens, rows = table.shape[1], acts.shape[0], shards[0].shape[1]
    chips = pairs // CORES
    chunk = pltpu.VMEM((CORES, tokens, 2 * BLOCK), jnp.bfloat16)
    packed = pltpu.VMEM((5 * rows, BLOCK), jnp.bfloat16)
    mask = pltpu.VMEM((chips, QUERIES, tokens), jnp.float32)
    operands = [
        pltpu.with_memory_space_constraint(a, pltpu.HBM) for a in (table, lengths, acts, grads, *shards)
    ]
    return pl.pallas_call(
        pack_kernel,
        out_shape=(packed, mask) + (chunk,) * chips,
        in_specs=[HBM] * len(operands),
        out_specs=(VMEM,) * (2 + chips),
        scratch_shapes=[
            pltpu.VMEM((rows, BLOCK), jnp.float32),
            pltpu.SMEM(table.shape, jnp.int32),
            pltpu.SMEM(lengths.shape, jnp.int32),
            pltpu.SemaphoreType.DMA((7 + 2 * pairs,)),
        ],
        compiler_params=pltpu.CompilerParams(vmem_limit_bytes=PACK_VMEM),
        cost_estimate=pl.CostEstimate(
            flops=0, bytes_accessed=pairs * tokens * BLOCK * 8, transcendentals=0
        ),
        name="pack",
    )(*operands)


def join_kernel(*refs):
    pieces, out = refs[:-1], refs[-1]
    rows = pieces[0].shape[0]
    for m, piece in enumerate(pieces):
        out[m * rows : (m + 1) * rows, :] = piece[...]


def join(pieces):
    rows = pieces[0].shape[0]
    return pl.pallas_call(
        join_kernel,
        out_shape=jax.ShapeDtypeStruct((len(pieces) * rows, BLOCK), jnp.bfloat16),
        in_specs=[VMEM] * len(pieces),
        out_specs=VMEM,
        compiler_params=pltpu.CompilerParams(vmem_limit_bytes=VMEM_BYTES),
        name="join",
    )(*pieces)


def pair_kernel(core, rows, chips, first_ref, last_ref, *refs):
    chunks, before = refs[:chips], refs[chips : -chips - 2]
    outs, full, precond = refs[-chips - 2 : -2], refs[-2], refs[-1]
    me = lax.axis_index("seq")
    if core:
        first_ref = first_ref.at[1 - lax.rem(lax.axis_index("blk"), CORES)]
    for odd, pieces in enumerate((first_ref, last_ref)):
        for i in range(pieces.shape[0] // (5 * rows)):
            place = pl.ds(pl.multiple_of((me ^ (2 * i + odd)) * rows, rows), rows)
            for part in range(5):
                start = (5 * i + part) * rows
                full[part, place, :] = pieces[start : start + rows, :]
    basis_act, basis_grad = full[0], full[1]
    qrot_acts = jnp.dot(full[2], basis_act, preferred_element_type=jnp.float32).astype(jnp.bfloat16)
    qrot_grads = jnp.dot(full[3], basis_grad, preferred_element_type=jnp.float32).astype(jnp.bfloat16)
    scale = 1.0 / (QTOK * (full[4].astype(jnp.float32) + DAMPING))
    for q in range(QUERIES):
        tokens = slice(q * QTOK, (q + 1) * QTOK)
        outer = lax.dot_general(
            qrot_grads[tokens], qrot_acts[tokens], TN, preferred_element_type=jnp.float32
        )
        precond[q] = (outer * scale).astype(jnp.bfloat16)
    tokens = chunks[0].shape[1]
    for m in range(0, chips, WIDTH):
        some = chunks[m : m + WIDTH]
        acts = jnp.concatenate([c[core, :, :BLOCK] for c in some], axis=0)
        grads = jnp.concatenate([c[core, :, BLOCK:] for c in some], axis=0)
        rot_acts = lax.dot_general(
            basis_act, acts, TT, preferred_element_type=jnp.float32
        ).astype(jnp.bfloat16)
        rot_grads = lax.dot_general(basis_grad, grads, TT, preferred_element_type=jnp.float32)
        sums = []
        for q in range(QUERIES):
            mixed = jnp.dot(precond[q], rot_acts, preferred_element_type=jnp.float32)
            sums.append(jnp.sum(mixed * rot_grads, axis=0, keepdims=True))
        scores = jnp.concatenate(sums, axis=0)
        for s in range(len(some)):
            part = scores[:, s * tokens : (s + 1) * tokens]
            if core:
                part = jnp.where(before[0][m + s] > 0, part + before[1 + m + s][...], 0.0)
            outs[m + s][...] = part


def pair_scores(core, first, last, chunks, before):
    chips, tokens = len(chunks), chunks[0].shape[1]
    rows = BLOCK // lax.axis_size("seq")
    operands = (first, last, *chunks, *before)
    return pl.pallas_call(
        functools.partial(pair_kernel, core, rows, chips),
        out_shape=(jax.ShapeDtypeStruct((QUERIES, tokens), jnp.float32),) * chips,
        in_specs=[VMEM] * len(operands),
        out_specs=(VMEM,) * chips,
        scratch_shapes=[
            pltpu.VMEM((5, BLOCK, BLOCK), jnp.bfloat16),
            pltpu.VMEM((QUERIES, BLOCK, BLOCK), jnp.bfloat16),
        ],
        compiler_params=pltpu.CompilerParams(vmem_limit_bytes=VMEM_BYTES),
        cost_estimate=pl.CostEstimate(
            flops=2 * chips * tokens * BLOCK * BLOCK * (QUERIES + 2),
            bytes_accessed=2 * BLOCK * (chips * tokens * 2 + BLOCK * (QUERIES + 2)),
            transcendentals=0,
        ),
        name="pair_scores",
    )(*operands)


def on_device(
    train_acts,
    train_grads,
    block_table,
    seq_lengths,
    query_acts,
    query_grads,
    basis_acts,
    basis_grads,
    eigenvalues,
):
    groups, chips = lax.axis_size("seq"), lax.axis_size("blk") // CORES
    packed, mask, *chunks = pack(
        block_table.T,
        seq_lengths,
        train_acts,
        train_grads,
        basis_acts,
        basis_grads,
        query_acts,
        query_grads,
        eigenvalues,
    )
    own = [packed]
    for m in range(1, groups):
        own.append(swap(own[m & (m - 1)], "seq", m & -m))
    far = sorted(range(1, chips), key=lambda m: -m.bit_count())
    chunks = [chunks[0]] + [swap(chunks[m], "blk", CORES * m) for m in far]
    first = join(own[::2])
    pairs = [list(range(c, c + CORES)) for c in range(0, chips * CORES, CORES)]
    both = lax.all_gather(first, "blk", axis=0, axis_index_groups=pairs)
    first, last, both, chunks = lax.optimization_barrier((first, own[1::2], both, chunks))
    chunks = [chunks[0]] + [chunks[1 + far.index(m)] for m in range(1, chips)]
    last = join(last)
    there = swap(last, "blk", 1)
    scores = pair_scores(0, first, last, chunks, ())
    scores = pair_scores(1, both, there, chunks, (mask, *scores))
    total = scores[0]
    for m in [k ^ (k >> 1) for k in range(1, chips)]:
        total = total + swap(scores[m], "blk", CORES * m)
    return total


def solution(mesh):
    in_specs = (
        P(("seq", "blk"), None),
        P(("seq", "blk"), None),
        P(),
        P(),
        P("blk", "seq", None),
        P("blk", "seq", None),
        P("blk", "seq", None),
        P("blk", "seq", None),
        P("blk", "seq", None),
    )
    out_specs = P(None, ("seq", "blk"))
    return jax.shard_map(
        on_device, mesh=mesh, in_specs=in_specs, out_specs=out_specs, check_vma=False
    )
```

```python
import functools

import jax
import jax.numpy as jnp
from jax import lax
from jax.experimental import pallas as pl
from jax.experimental.pallas import tpu as pltpu
from jax.sharding import PartitionSpec as P

BLOCK = 256
SEQ_LEN = 1024
QUERIES = 8
QTOK = 32
DAMPING = 0.1
CORES = 2
WIDTH = 4
PACK_VMEM = 16 * 1024 * 1024
VMEM_BYTES = 24 * 1024 * 1024

VMEM = pl.BlockSpec(memory_space=pltpu.VMEM)
HBM = pl.BlockSpec(memory_space=pltpu.HBM)
TT = (((0,), (1,)), ((), ()))
TN = (((0,), (0,)), ((), ()))


def swap(array, axis, bits):
    return lax.ppermute(array, axis, [(i, i ^ bits) for i in range(lax.axis_size(axis))])


def valid_mask(lengths, sequences, start, shape):
    position = start + lax.broadcasted_iota(jnp.int32, shape, 1)
    low = start // SEQ_LEN
    valid = jnp.zeros(shape, jnp.float32)
    for s in range((shape[1] + SEQ_LEN - 2) // SEQ_LEN + 1):
        sequence = jnp.minimum(low + s, sequences - 1)
        offset = position - sequence * SEQ_LEN
        valid = jnp.where((offset >= 0) & (offset < lengths[sequence]), 1.0, valid)
    return valid


def copy_blocks(table, distances, acts_ref, grads_ref, chunks, sem):
    me = lax.axis_index("blk")
    copies = []
    for m, chunk in zip(distances, chunks):
        for core in range(CORES):
            owner = me ^ (CORES * m + core)
            for half, (source, row) in enumerate(((acts_ref, 1), (grads_ref, 0))):
                start = pl.multiple_of(table[row, owner] * BLOCK, BLOCK)
                copy = pltpu.make_async_copy(
                    source.at[:, pl.ds(start, BLOCK)],
                    chunk.at[core, :, pl.ds(half * BLOCK, BLOCK)],
                    sem.at[len(copies)],
                )
                copy.start()
                copies.append(copy)
    return copies


def blocks_kernel(distances, table_ref, acts_ref, grads_ref, *refs):
    chunks, (table, sem, table_sem) = refs[:-3], refs[-3:]
    copy = pltpu.make_async_copy(table_ref, table, table_sem)
    copy.start()
    copy.wait()
    for copy in copy_blocks(table, distances, acts_ref, grads_ref, chunks, sem):
        copy.wait()


def take_blocks(distances, table, acts, grads):
    tokens = acts.shape[0]
    operands = [pltpu.with_memory_space_constraint(a, pltpu.HBM) for a in (table, acts, grads)]
    return pl.pallas_call(
        functools.partial(blocks_kernel, distances),
        out_shape=(pltpu.VMEM((CORES, tokens, 2 * BLOCK), jnp.bfloat16),) * len(distances),
        in_specs=[HBM] * 3,
        out_specs=(VMEM,) * len(distances),
        scratch_shapes=[
            pltpu.SMEM(table.shape, jnp.int32),
            pltpu.SemaphoreType.DMA((2 * CORES * len(distances),)),
            pltpu.SemaphoreType.DMA,
        ],
        compiler_params=pltpu.CompilerParams(vmem_limit_bytes=VMEM_BYTES),
        name="take_blocks",
    )(*operands)


def pack_kernel(distances, table_ref, lengths_ref, acts_ref, grads_ref, *refs):
    shards, packed_ref, mask_ref = refs[:5], refs[5], refs[6]
    chunks, (raw_eigen, table, lengths, sem) = refs[7:-4], refs[-4:]
    me = lax.axis_index("blk")
    rows, tokens = raw_eigen.shape[0], acts_ref.shape[0]
    scalars = [
        pltpu.make_async_copy(table_ref, table, sem.at[0]),
        pltpu.make_async_copy(lengths_ref, lengths, sem.at[1]),
    ]
    weights = []
    for part, shard in enumerate(shards):
        target = raw_eigen if part == 4 else packed_ref.at[pl.ds(part * rows, rows), :]
        weights.append(pltpu.make_async_copy(shard.at[0], target, sem.at[2 + part]))
    for copy in scalars + weights:
        copy.start()
    scalars[0].wait()
    copies = copy_blocks(table, distances, acts_ref, grads_ref, chunks, sem.at[pl.ds(7, 2 * CORES)])
    scalars[1].wait()
    group = lax.axis_index("seq") * lax.axis_size("blk")
    for m in range(mask_ref.shape[0]):
        start = (group + (me ^ (CORES * m))) * tokens
        mask_ref[m] = valid_mask(lengths, lengths_ref.shape[0], start, mask_ref.shape[1:])
    for copy in weights:
        copy.wait()
    packed_ref[4 * rows :, :] = raw_eigen[...].astype(jnp.bfloat16)
    for copy in copies:
        copy.wait()


def pack(distances, table, lengths, acts, grads, *shards):
    pairs, tokens, rows = table.shape[1], acts.shape[0], shards[0].shape[1]
    chips = pairs // CORES
    chunk = pltpu.VMEM((CORES, tokens, 2 * BLOCK), jnp.bfloat16)
    packed = pltpu.VMEM((5 * rows, BLOCK), jnp.bfloat16)
    mask = pltpu.VMEM((chips, QUERIES, tokens), jnp.float32)
    operands = [
        pltpu.with_memory_space_constraint(a, pltpu.HBM) for a in (table, lengths, acts, grads, *shards)
    ]
    return pl.pallas_call(
        functools.partial(pack_kernel, distances),
        out_shape=(packed, mask) + (chunk,) * len(distances),
        in_specs=[HBM] * len(operands),
        out_specs=(VMEM,) * (2 + len(distances)),
        scratch_shapes=[
            pltpu.VMEM((rows, BLOCK), jnp.float32),
            pltpu.SMEM(table.shape, jnp.int32),
            pltpu.SMEM(lengths.shape, jnp.int32),
            pltpu.SemaphoreType.DMA((7 + 2 * pairs,)),
        ],
        compiler_params=pltpu.CompilerParams(vmem_limit_bytes=PACK_VMEM),
        cost_estimate=pl.CostEstimate(
            flops=0, bytes_accessed=pairs * tokens * BLOCK * 8, transcendentals=0
        ),
        name="pack",
    )(*operands)


def join_kernel(*refs):
    pieces, out = refs[:-1], refs[-1]
    rows = pieces[0].shape[0]
    for m, piece in enumerate(pieces):
        out[m * rows : (m + 1) * rows, :] = piece[...]


def join(pieces):
    rows = pieces[0].shape[0]
    return pl.pallas_call(
        join_kernel,
        out_shape=jax.ShapeDtypeStruct((len(pieces) * rows, BLOCK), jnp.bfloat16),
        in_specs=[VMEM] * len(pieces),
        out_specs=VMEM,
        compiler_params=pltpu.CompilerParams(vmem_limit_bytes=VMEM_BYTES),
        name="join",
    )(*pieces)


def pair_kernel(core, rows, chips, first_ref, last_ref, *refs):
    chunks, before = refs[:chips], refs[chips : -chips - 2]
    outs, full, precond = refs[-chips - 2 : -2], refs[-2], refs[-1]
    me = lax.axis_index("seq")
    if core:
        first_ref = first_ref.at[1 - lax.rem(lax.axis_index("blk"), CORES)]
    m = 0
    for pieces in (first_ref, last_ref):
        for first in range(0, pieces.shape[0], 5 * rows):
            place = pl.ds(pl.multiple_of((me ^ m) * rows, rows), rows)
            for part in range(5):
                start = first + part * rows
                full[part, place, :] = pieces[start : start + rows, :]
            m += 1
    basis_act, basis_grad = full[0], full[1]
    qrot_acts = jnp.dot(full[2], basis_act, preferred_element_type=jnp.float32).astype(jnp.bfloat16)
    qrot_grads = jnp.dot(full[3], basis_grad, preferred_element_type=jnp.float32).astype(jnp.bfloat16)
    scale = 1.0 / (QTOK * (full[4].astype(jnp.float32) + DAMPING))
    tokens = chunks[0].shape[1]
    for m in range(0, chips, WIDTH):
        some = chunks[m : m + WIDTH]
        acts = jnp.concatenate([c[core, :, :BLOCK] for c in some], axis=0)
        grads = jnp.concatenate([c[core, :, BLOCK:] for c in some], axis=0)
        rot_acts = lax.dot_general(
            basis_act, acts, TT, preferred_element_type=jnp.float32
        ).astype(jnp.bfloat16)
        rot_grads = lax.dot_general(basis_grad, grads, TT, preferred_element_type=jnp.float32)
        if m == 0:
            for q in range(QUERIES):
                rows_q = slice(q * QTOK, (q + 1) * QTOK)
                outer = lax.dot_general(
                    qrot_grads[rows_q], qrot_acts[rows_q], TN, preferred_element_type=jnp.float32
                )
                precond[q] = (outer * scale).astype(jnp.bfloat16)
        sums = []
        for q in range(QUERIES):
            mixed = jnp.dot(precond[q], rot_acts, preferred_element_type=jnp.float32)
            sums.append(jnp.sum(mixed * rot_grads, axis=0, keepdims=True))
        scores = jnp.concatenate(sums, axis=0)
        for s in range(len(some)):
            part = scores[:, s * tokens : (s + 1) * tokens]
            if core:
                part = jnp.where(before[0][m + s] > 0, part + before[1 + m + s][...], 0.0)
            outs[m + s][...] = part


def pair_scores(core, first, last, chunks, before):
    chips, tokens = len(chunks), chunks[0].shape[1]
    rows = BLOCK // lax.axis_size("seq")
    operands = (first, last, *chunks, *before)
    return pl.pallas_call(
        functools.partial(pair_kernel, core, rows, chips),
        out_shape=(jax.ShapeDtypeStruct((QUERIES, tokens), jnp.float32),) * chips,
        in_specs=[VMEM] * len(operands),
        out_specs=(VMEM,) * chips,
        scratch_shapes=[
            pltpu.VMEM((5, BLOCK, BLOCK), jnp.bfloat16),
            pltpu.VMEM((QUERIES, BLOCK, BLOCK), jnp.bfloat16),
        ],
        compiler_params=pltpu.CompilerParams(vmem_limit_bytes=VMEM_BYTES),
        cost_estimate=pl.CostEstimate(
            flops=2 * chips * tokens * BLOCK * BLOCK * (QUERIES + 2),
            bytes_accessed=2 * BLOCK * (chips * tokens * 2 + BLOCK * (QUERIES + 2)),
            transcendentals=0,
        ),
        name="pair_scores",
    )(*operands)


def on_device(
    train_acts,
    train_grads,
    block_table,
    seq_lengths,
    query_acts,
    query_grads,
    basis_acts,
    basis_grads,
    eigenvalues,
):
    groups, chips = lax.axis_size("seq"), lax.axis_size("blk") // CORES
    far = sorted(range(1, chips), key=lambda m: -m.bit_count())
    packed, mask, *ahead = pack(
        far[:1],
        block_table.T,
        seq_lengths,
        train_acts,
        train_grads,
        basis_acts,
        basis_grads,
        query_acts,
        query_grads,
        eigenvalues,
    )
    own = [packed]
    for m in range(1, groups):
        own.append(swap(own[m & (m - 1)], "seq", m & -m))
    others = far[1:] + [0]
    chunks = dict(zip(far[:1], ahead)) | dict(
        zip(others, take_blocks(others, block_table.T, train_acts, train_grads))
    )
    chunks = [chunks[0]] + [swap(chunks[m], "blk", CORES * m) for m in far]
    early, chunks[1] = lax.optimization_barrier((own[:-1], chunks[1]))
    first = join(early)
    pairs = [list(range(c, c + CORES)) for c in range(0, chips * CORES, CORES)]
    both = lax.all_gather(first, "blk", axis=0, axis_index_groups=pairs)
    first, last, both, chunks = lax.optimization_barrier((first, own[-1], both, chunks))
    chunks = [chunks[0]] + [chunks[1 + far.index(m)] for m in range(1, chips)]
    there = swap(last, "blk", 1)
    scores = pair_scores(0, first, last, chunks, ())
    scores = pair_scores(1, both, there, chunks, (mask, *scores))
    total = scores[0]
    for m in [k ^ (k >> 1) for k in range(1, chips)]:
        total = total + swap(scores[m], "blk", CORES * m)
    return total


def solution(mesh):
    in_specs = (
        P(("seq", "blk"), None),
        P(("seq", "blk"), None),
        P(),
        P(),
        P("blk", "seq", None),
        P("blk", "seq", None),
        P("blk", "seq", None),
        P("blk", "seq", None),
        P("blk", "seq", None),
    )
    out_specs = P(None, ("seq", "blk"))
    return jax.shard_map(
        on_device, mesh=mesh, in_specs=in_specs, out_specs=out_specs, check_vma=False
    )
```

```python
import functools

import jax
import jax.numpy as jnp
from jax import lax
from jax.experimental import pallas as pl
from jax.experimental.pallas import tpu as pltpu
from jax.sharding import PartitionSpec as P

BLOCK = 256
SEQ_LEN = 1024
QUERIES = 8
QTOK = 32
DAMPING = 0.1
CORES = 2
WIDTH = 4
PACK_VMEM = 16 * 1024 * 1024
VMEM_BYTES = 24 * 1024 * 1024

VMEM = pl.BlockSpec(memory_space=pltpu.VMEM)
HBM = pl.BlockSpec(memory_space=pltpu.HBM)
TT = (((0,), (1,)), ((), ()))
TN = (((0,), (0,)), ((), ()))


def swap(array, axis, bits):
    return lax.ppermute(array, axis, [(i, i ^ bits) for i in range(lax.axis_size(axis))])


def valid_mask(lengths, sequences, start, shape):
    position = start + lax.broadcasted_iota(jnp.int32, shape, 1)
    low = start // SEQ_LEN
    valid = jnp.zeros(shape, jnp.float32)
    for s in range((shape[1] + SEQ_LEN - 2) // SEQ_LEN + 1):
        sequence = jnp.minimum(low + s, sequences - 1)
        offset = position - sequence * SEQ_LEN
        valid = jnp.where((offset >= 0) & (offset < lengths[sequence]), 1.0, valid)
    return valid


def copy_blocks(table, distances, acts_ref, grads_ref, chunks, sem):
    me = lax.axis_index("blk")
    copies = []
    for m, chunk in zip(distances, chunks):
        for core in range(CORES):
            owner = me ^ (CORES * m + core)
            for half, (source, row) in enumerate(((acts_ref, 1), (grads_ref, 0))):
                start = pl.multiple_of(table[row, owner] * BLOCK, BLOCK)
                copy = pltpu.make_async_copy(
                    source.at[:, pl.ds(start, BLOCK)],
                    chunk.at[core, :, pl.ds(half * BLOCK, BLOCK)],
                    sem.at[len(copies)],
                )
                copy.start()
                copies.append(copy)
    return copies


def blocks_kernel(distances, table_ref, acts_ref, grads_ref, *refs):
    chunks, (table, sem, table_sem) = refs[:-3], refs[-3:]
    copy = pltpu.make_async_copy(table_ref, table, table_sem)
    copy.start()
    copy.wait()
    for copy in copy_blocks(table, distances, acts_ref, grads_ref, chunks, sem):
        copy.wait()


def take_blocks(distances, table, acts, grads):
    tokens = acts.shape[0]
    operands = [pltpu.with_memory_space_constraint(a, pltpu.HBM) for a in (table, acts, grads)]
    return pl.pallas_call(
        functools.partial(blocks_kernel, distances),
        out_shape=(pltpu.VMEM((CORES, tokens, 2 * BLOCK), jnp.bfloat16),) * len(distances),
        in_specs=[HBM] * 3,
        out_specs=(VMEM,) * len(distances),
        scratch_shapes=[
            pltpu.SMEM(table.shape, jnp.int32),
            pltpu.SemaphoreType.DMA((2 * CORES * len(distances),)),
            pltpu.SemaphoreType.DMA,
        ],
        compiler_params=pltpu.CompilerParams(vmem_limit_bytes=VMEM_BYTES),
        name="take_blocks",
    )(*operands)


def pack_kernel(distances, table_ref, lengths_ref, acts_ref, grads_ref, *refs):
    shards, packed_ref, mask_ref = refs[:5], refs[5], refs[6]
    chunks, (raw_eigen, table, lengths, sem) = refs[7:-4], refs[-4:]
    me = lax.axis_index("blk")
    rows, tokens = raw_eigen.shape[0], acts_ref.shape[0]
    scalars = [
        pltpu.make_async_copy(table_ref, table, sem.at[0]),
        pltpu.make_async_copy(lengths_ref, lengths, sem.at[1]),
    ]
    weights = []
    for part, shard in enumerate(shards):
        target = raw_eigen if part == 4 else packed_ref.at[pl.ds(part * rows, rows), :]
        weights.append(pltpu.make_async_copy(shard.at[0], target, sem.at[2 + part]))
    for copy in scalars + weights:
        copy.start()
    scalars[0].wait()
    copies = copy_blocks(table, distances, acts_ref, grads_ref, chunks, sem.at[pl.ds(7, 2 * CORES)])
    scalars[1].wait()
    group = lax.axis_index("seq") * lax.axis_size("blk")
    for m in range(mask_ref.shape[0]):
        start = (group + (me ^ (CORES * m))) * tokens
        mask_ref[m] = valid_mask(lengths, lengths_ref.shape[0], start, mask_ref.shape[1:])
    for copy in weights:
        copy.wait()
    packed_ref[4 * rows :, :] = raw_eigen[...].astype(jnp.bfloat16)
    for copy in copies:
        copy.wait()


def pack(distances, table, lengths, acts, grads, *shards):
    pairs, tokens, rows = table.shape[1], acts.shape[0], shards[0].shape[1]
    chips = pairs // CORES
    chunk = pltpu.VMEM((CORES, tokens, 2 * BLOCK), jnp.bfloat16)
    packed = pltpu.VMEM((5 * rows, BLOCK), jnp.bfloat16)
    mask = pltpu.VMEM((chips, QUERIES, tokens), jnp.float32)
    operands = [
        pltpu.with_memory_space_constraint(a, pltpu.HBM) for a in (table, lengths, acts, grads, *shards)
    ]
    return pl.pallas_call(
        functools.partial(pack_kernel, distances),
        out_shape=(packed, mask) + (chunk,) * len(distances),
        in_specs=[HBM] * len(operands),
        out_specs=(VMEM,) * (2 + len(distances)),
        scratch_shapes=[
            pltpu.VMEM((rows, BLOCK), jnp.float32),
            pltpu.SMEM(table.shape, jnp.int32),
            pltpu.SMEM(lengths.shape, jnp.int32),
            pltpu.SemaphoreType.DMA((7 + 2 * pairs,)),
        ],
        compiler_params=pltpu.CompilerParams(vmem_limit_bytes=PACK_VMEM),
        cost_estimate=pl.CostEstimate(
            flops=0, bytes_accessed=pairs * tokens * BLOCK * 8, transcendentals=0
        ),
        name="pack",
    )(*operands)


def join_kernel(*refs):
    pieces, out = refs[:-1], refs[-1]
    rows = pieces[0].shape[0]
    for m, piece in enumerate(pieces):
        out[m * rows : (m + 1) * rows, :] = piece[...]


def join(pieces):
    rows = pieces[0].shape[0]
    return pl.pallas_call(
        join_kernel,
        out_shape=jax.ShapeDtypeStruct((len(pieces) * rows, BLOCK), jnp.bfloat16),
        in_specs=[VMEM] * len(pieces),
        out_specs=VMEM,
        compiler_params=pltpu.CompilerParams(vmem_limit_bytes=VMEM_BYTES),
        name="join",
    )(*pieces)


def pair_kernel(core, rows, chips, sources, first_ref, last_ref, *refs):
    chunks, before = refs[:chips], refs[chips : -chips - 2]
    outs, full, precond = refs[-chips - 2 : -2], refs[-2], refs[-1]
    me = lax.axis_index("seq")
    if core:
        first_ref = first_ref.at[1 - lax.rem(lax.axis_index("blk"), CORES)]
    whose = iter(sources)
    for pieces in (first_ref, last_ref):
        for first in range(0, pieces.shape[0], 5 * rows):
            place = pl.ds(pl.multiple_of(next(whose)(me) * rows, rows), rows)
            for part in range(5):
                start = first + part * rows
                full[part, place, :] = pieces[start : start + rows, :]
    basis_act, basis_grad = full[0], full[1]
    qrot_acts = jnp.dot(full[2], basis_act, preferred_element_type=jnp.float32).astype(jnp.bfloat16)
    qrot_grads = jnp.dot(full[3], basis_grad, preferred_element_type=jnp.float32).astype(jnp.bfloat16)
    scale = 1.0 / (QTOK * (full[4].astype(jnp.float32) + DAMPING))
    tokens = chunks[0].shape[1]
    for m in range(0, chips, WIDTH):
        some = chunks[m : m + WIDTH]
        acts = jnp.concatenate([c[core, :, :BLOCK] for c in some], axis=0)
        grads = jnp.concatenate([c[core, :, BLOCK:] for c in some], axis=0)
        rot_acts = lax.dot_general(
            basis_act, acts, TT, preferred_element_type=jnp.float32
        ).astype(jnp.bfloat16)
        rot_grads = lax.dot_general(basis_grad, grads, TT, preferred_element_type=jnp.float32)
        if m == 0:
            for q in range(QUERIES):
                rows_q = slice(q * QTOK, (q + 1) * QTOK)
                outer = lax.dot_general(
                    qrot_grads[rows_q], qrot_acts[rows_q], TN, preferred_element_type=jnp.float32
                )
                precond[q] = (outer * scale).astype(jnp.bfloat16)
        sums = []
        for q in range(QUERIES):
            mixed = jnp.dot(precond[q], rot_acts, preferred_element_type=jnp.float32)
            sums.append(jnp.sum(mixed * rot_grads, axis=0, keepdims=True))
        scores = jnp.concatenate(sums, axis=0)
        for s in range(len(some)):
            part = scores[:, s * tokens : (s + 1) * tokens]
            if core:
                part = jnp.where(before[0][m + s] > 0, part + before[1 + m + s][...], 0.0)
            outs[m + s][...] = part


def pair_scores(core, sources, first, last, chunks, before):
    chips, tokens = len(chunks), chunks[0].shape[1]
    rows = BLOCK // lax.axis_size("seq")
    operands = (first, last, *chunks, *before)
    return pl.pallas_call(
        functools.partial(pair_kernel, core, rows, chips, sources),
        out_shape=(jax.ShapeDtypeStruct((QUERIES, tokens), jnp.float32),) * chips,
        in_specs=[VMEM] * len(operands),
        out_specs=(VMEM,) * chips,
        scratch_shapes=[
            pltpu.VMEM((5, BLOCK, BLOCK), jnp.bfloat16),
            pltpu.VMEM((QUERIES, BLOCK, BLOCK), jnp.bfloat16),
        ],
        compiler_params=pltpu.CompilerParams(vmem_limit_bytes=VMEM_BYTES),
        cost_estimate=pl.CostEstimate(
            flops=2 * chips * tokens * BLOCK * BLOCK * (QUERIES + 2),
            bytes_accessed=2 * BLOCK * (chips * tokens * 2 + BLOCK * (QUERIES + 2)),
            transcendentals=0,
        ),
        name="pair_scores",
    )(*operands)


def on_device(
    train_acts,
    train_grads,
    block_table,
    seq_lengths,
    query_acts,
    query_grads,
    basis_acts,
    basis_grads,
    eigenvalues,
):
    groups, chips = lax.axis_size("seq"), lax.axis_size("blk") // CORES
    far = sorted(range(1, chips), key=lambda m: -m.bit_count())
    packed, mask, *ahead = pack(
        far[:1],
        block_table.T,
        seq_lengths,
        train_acts,
        train_grads,
        basis_acts,
        basis_grads,
        query_acts,
        query_grads,
        eigenvalues,
    )
    if groups == 4:
        ahead_of = lax.ppermute(packed, "seq", [(0, 2), (2, 3), (3, 1), (1, 0)])
        behind = lax.ppermute(packed, "seq", [(2, 0), (3, 2), (1, 3), (0, 1)])
        me = lax.axis_index("seq")
        relay = jnp.where((me == 1) | (me == 2), ahead_of, behind)
        own = [packed, ahead_of, behind, swap(relay, "seq", 1)]
        sources = [
            lambda me: me,
            lambda me: lax.rem(2 * me + 1, 5),
            lambda me: lax.rem(3 * me + 2, 5),
            lambda me: 3 - me,
        ]
    else:
        own = [packed]
        for m in range(1, groups):
            own.append(swap(own[m & (m - 1)], "seq", m & -m))
        sources = [lambda me, m=m: me ^ m for m in range(groups)]
    others = far[1:] + [0]
    chunks = dict(zip(far[:1], ahead)) | dict(
        zip(others, take_blocks(others, block_table.T, train_acts, train_grads))
    )
    chunks = [chunks[0]] + [swap(chunks[m], "blk", CORES * m) for m in far]
    early, chunks[1] = lax.optimization_barrier((own[:-1], chunks[1]))
    first = join(early)
    pairs = [list(range(c, c + CORES)) for c in range(0, chips * CORES, CORES)]
    both = lax.all_gather(first, "blk", axis=0, axis_index_groups=pairs)
    first, last, both, chunks = lax.optimization_barrier((first, own[-1], both, chunks))
    chunks = [chunks[0]] + [chunks[1 + far.index(m)] for m in range(1, chips)]
    there = swap(last, "blk", 1)
    scores = pair_scores(0, sources, first, last, chunks, ())
    scores = pair_scores(1, sources, both, there, chunks, (mask, *scores))
    total = scores[0]
    for m in [k ^ (k >> 1) for k in range(1, chips)]:
        total = total + swap(scores[m], "blk", CORES * m)
    return total


def solution(mesh):
    in_specs = (
        P(("seq", "blk"), None),
        P(("seq", "blk"), None),
        P(),
        P(),
        P("blk", "seq", None),
        P("blk", "seq", None),
        P("blk", "seq", None),
        P("blk", "seq", None),
        P("blk", "seq", None),
    )
    out_specs = P(None, ("seq", "blk"))
    return jax.shard_map(
        on_device, mesh=mesh, in_specs=in_specs, out_specs=out_specs, check_vma=False
    )
```

```python
import functools

import jax
import jax.numpy as jnp
from jax import lax
from jax.experimental import pallas as pl
from jax.experimental.pallas import tpu as pltpu
from jax.sharding import PartitionSpec as P

BLOCK = 256
SEQ_LEN = 1024
QUERIES = 8
QTOK = 32
DAMPING = 0.1
CORES = 2
WIDTH = 4
PACK_VMEM = 16 * 1024 * 1024
VMEM_BYTES = 24 * 1024 * 1024

VMEM = pl.BlockSpec(memory_space=pltpu.VMEM)
HBM = pl.BlockSpec(memory_space=pltpu.HBM)
TT = (((0,), (1,)), ((), ()))
TN = (((0,), (0,)), ((), ()))


def swap(array, axis, bits):
    return lax.ppermute(array, axis, [(i, i ^ bits) for i in range(lax.axis_size(axis))])


def valid_mask(lengths, sequences, start, shape):
    position = start + lax.broadcasted_iota(jnp.int32, shape, 1)
    low = start // SEQ_LEN
    valid = jnp.zeros(shape, jnp.float32)
    for s in range((shape[1] + SEQ_LEN - 2) // SEQ_LEN + 1):
        sequence = jnp.minimum(low + s, sequences - 1)
        offset = position - sequence * SEQ_LEN
        valid = jnp.where((offset >= 0) & (offset < lengths[sequence]), 1.0, valid)
    return valid


def copy_blocks(table, distances, acts_ref, grads_ref, chunks, sem):
    me = lax.axis_index("blk")
    copies = []
    for m, chunk in zip(distances, chunks):
        for core in range(CORES):
            owner = me ^ (CORES * m + core)
            for half, (source, row) in enumerate(((acts_ref, 1), (grads_ref, 0))):
                start = pl.multiple_of(table[row, owner] * BLOCK, BLOCK)
                copy = pltpu.make_async_copy(
                    source.at[:, pl.ds(start, BLOCK)],
                    chunk.at[core, :, pl.ds(half * BLOCK, BLOCK)],
                    sem.at[len(copies)],
                )
                copy.start()
                copies.append(copy)
    return copies


def blocks_kernel(distances, table_ref, lengths_ref, acts_ref, grads_ref, mask_ref, *refs):
    chunks, (table, lengths, sem) = refs[:-3], refs[-3:]
    count = 2 * CORES * len(distances)
    scalars = [
        pltpu.make_async_copy(table_ref, table, sem.at[count]),
        pltpu.make_async_copy(lengths_ref, lengths, sem.at[count + 1]),
    ]
    for copy in scalars:
        copy.start()
    scalars[0].wait()
    copies = copy_blocks(table, distances, acts_ref, grads_ref, chunks, sem)
    scalars[1].wait()
    me = lax.axis_index("blk")
    group = lax.axis_index("seq") * lax.axis_size("blk")
    chips, _, tokens = mask_ref.shape
    for m in range(chips):
        start = (group + (me ^ (CORES * m))) * tokens
        mask_ref[m] = valid_mask(lengths, lengths_ref.shape[0], start, mask_ref.shape[1:])
    for copy in copies:
        copy.wait()


def take_blocks(distances, table, lengths, acts, grads):
    tokens, chips = acts.shape[0], table.shape[1] // CORES
    operands = [
        pltpu.with_memory_space_constraint(a, pltpu.HBM) for a in (table, lengths, acts, grads)
    ]
    return pl.pallas_call(
        functools.partial(blocks_kernel, distances),
        out_shape=(pltpu.VMEM((chips, QUERIES, tokens), jnp.float32),)
        + (pltpu.VMEM((CORES, tokens, 2 * BLOCK), jnp.bfloat16),) * len(distances),
        in_specs=[HBM] * 4,
        out_specs=(VMEM,) * (1 + len(distances)),
        scratch_shapes=[
            pltpu.SMEM(table.shape, jnp.int32),
            pltpu.SMEM(lengths.shape, jnp.int32),
            pltpu.SemaphoreType.DMA((2 * CORES * len(distances) + 2,)),
        ],
        compiler_params=pltpu.CompilerParams(vmem_limit_bytes=VMEM_BYTES),
        name="take_blocks",
    )(*operands)


def pack_kernel(distances, table_ref, acts_ref, grads_ref, *refs):
    shards, packed_ref = refs[:5], refs[5]
    chunks, (raw_eigen, table, sem) = refs[6:-3], refs[-3:]
    rows = raw_eigen.shape[0]
    fetch = pltpu.make_async_copy(table_ref, table, sem.at[0])
    fetch.start()
    weights = []
    for part, shard in enumerate(shards):
        target = raw_eigen if part == 4 else packed_ref.at[pl.ds(part * rows, rows), :]
        weights.append(pltpu.make_async_copy(shard.at[0], target, sem.at[1 + part]))
    for copy in weights:
        copy.start()
    fetch.wait()
    copies = copy_blocks(table, distances, acts_ref, grads_ref, chunks, sem.at[pl.ds(6, 2 * CORES)])
    for copy in weights:
        copy.wait()
    packed_ref[4 * rows :, :] = raw_eigen[...].astype(jnp.bfloat16)
    for copy in copies:
        copy.wait()


def pack(distances, table, acts, grads, *shards):
    tokens, rows = acts.shape[0], shards[0].shape[1]
    chunk = pltpu.VMEM((CORES, tokens, 2 * BLOCK), jnp.bfloat16)
    packed = pltpu.VMEM((5 * rows, BLOCK), jnp.bfloat16)
    operands = [pltpu.with_memory_space_constraint(a, pltpu.HBM) for a in (table, acts, grads, *shards)]
    return pl.pallas_call(
        functools.partial(pack_kernel, distances),
        out_shape=(packed,) + (chunk,) * len(distances),
        in_specs=[HBM] * len(operands),
        out_specs=(VMEM,) * (1 + len(distances)),
        scratch_shapes=[
            pltpu.VMEM((rows, BLOCK), jnp.float32),
            pltpu.SMEM(table.shape, jnp.int32),
            pltpu.SemaphoreType.DMA((6 + 2 * CORES * len(distances),)),
        ],
        compiler_params=pltpu.CompilerParams(vmem_limit_bytes=PACK_VMEM),
        name="pack",
    )(*operands)


def join_kernel(*refs):
    pieces, out = refs[:-1], refs[-1]
    rows = pieces[0].shape[0]
    for m, piece in enumerate(pieces):
        out[m * rows : (m + 1) * rows, :] = piece[...]


def join(pieces):
    rows = pieces[0].shape[0]
    return pl.pallas_call(
        join_kernel,
        out_shape=jax.ShapeDtypeStruct((len(pieces) * rows, BLOCK), jnp.bfloat16),
        in_specs=[VMEM] * len(pieces),
        out_specs=VMEM,
        compiler_params=pltpu.CompilerParams(vmem_limit_bytes=VMEM_BYTES),
        name="join",
    )(*pieces)


def pair_kernel(core, rows, chips, first_ref, last_ref, *refs):
    chunks, before = refs[:chips], refs[chips : -chips - 2]
    outs, full, precond = refs[-chips - 2 : -2], refs[-2], refs[-1]
    me = lax.axis_index("seq")
    if core:
        first_ref = first_ref.at[1 - lax.rem(lax.axis_index("blk"), CORES)]
    m = 0
    for pieces in (first_ref, last_ref):
        for first in range(0, pieces.shape[0], 5 * rows):
            place = pl.ds(pl.multiple_of((me ^ m) * rows, rows), rows)
            for part in range(5):
                start = first + part * rows
                full[part, place, :] = pieces[start : start + rows, :]
            m += 1
    basis_act, basis_grad = full[0], full[1]
    qrot_acts = jnp.dot(full[2], basis_act, preferred_element_type=jnp.float32).astype(jnp.bfloat16)
    qrot_grads = jnp.dot(full[3], basis_grad, preferred_element_type=jnp.float32).astype(jnp.bfloat16)
    scale = 1.0 / (QTOK * (full[4].astype(jnp.float32) + DAMPING))
    tokens = chunks[0].shape[1]
    for m in range(0, chips, WIDTH):
        some = chunks[m : m + WIDTH]
        acts = jnp.concatenate([c[core, :, :BLOCK] for c in some], axis=0)
        grads = jnp.concatenate([c[core, :, BLOCK:] for c in some], axis=0)
        rot_acts = lax.dot_general(
            basis_act, acts, TT, preferred_element_type=jnp.float32
        ).astype(jnp.bfloat16)
        rot_grads = lax.dot_general(basis_grad, grads, TT, preferred_element_type=jnp.float32)
        if m == 0:
            for q in range(QUERIES):
                rows_q = slice(q * QTOK, (q + 1) * QTOK)
                outer = lax.dot_general(
                    qrot_grads[rows_q], qrot_acts[rows_q], TN, preferred_element_type=jnp.float32
                )
                precond[q] = (outer * scale).astype(jnp.bfloat16)
        sums = []
        for q in range(QUERIES):
            mixed = jnp.dot(precond[q], rot_acts, preferred_element_type=jnp.float32)
            sums.append(jnp.sum(mixed * rot_grads, axis=0, keepdims=True))
        scores = jnp.concatenate(sums, axis=0)
        for s in range(len(some)):
            part = scores[:, s * tokens : (s + 1) * tokens]
            if core:
                part = jnp.where(before[0][m + s] > 0, part + before[1 + m + s][...], 0.0)
            outs[m + s][...] = part


def pair_scores(core, first, last, chunks, before):
    chips, tokens = len(chunks), chunks[0].shape[1]
    rows = BLOCK // lax.axis_size("seq")
    operands = (first, last, *chunks, *before)
    return pl.pallas_call(
        functools.partial(pair_kernel, core, rows, chips),
        out_shape=(jax.ShapeDtypeStruct((QUERIES, tokens), jnp.float32),) * chips,
        in_specs=[VMEM] * len(operands),
        out_specs=(VMEM,) * chips,
        scratch_shapes=[
            pltpu.VMEM((5, BLOCK, BLOCK), jnp.bfloat16),
            pltpu.VMEM((QUERIES, BLOCK, BLOCK), jnp.bfloat16),
        ],
        compiler_params=pltpu.CompilerParams(vmem_limit_bytes=VMEM_BYTES),
        cost_estimate=pl.CostEstimate(
            flops=2 * chips * tokens * BLOCK * BLOCK * (QUERIES + 2),
            bytes_accessed=2 * BLOCK * (chips * tokens * 2 + BLOCK * (QUERIES + 2)),
            transcendentals=0,
        ),
        name="pair_scores",
    )(*operands)


def on_device(
    train_acts,
    train_grads,
    block_table,
    seq_lengths,
    query_acts,
    query_grads,
    basis_acts,
    basis_grads,
    eigenvalues,
):
    groups, chips = lax.axis_size("seq"), lax.axis_size("blk") // CORES
    far = sorted(range(1, chips), key=lambda m: -m.bit_count())
    packed, *ahead = pack(
        far[:1],
        block_table.T,
        train_acts,
        train_grads,
        basis_acts,
        basis_grads,
        query_acts,
        query_grads,
        eigenvalues,
    )
    own = [packed]
    for m in range(1, groups):
        piece = own[m & (m - 1)]
        if m & (m - 1):
            piece = jnp.where(lax.axis_index("seq") >= 0, piece, packed)
        own.append(swap(piece, "seq", m & -m))
    others = far[1:] + [0]
    mask, *later = take_blocks(others, block_table.T, seq_lengths, train_acts, train_grads)
    chunks = dict(zip(far[:1] + others, ahead + later))
    chunks = [chunks[0]] + [swap(chunks[m], "blk", CORES * m) for m in far]
    early, chunks[1] = lax.optimization_barrier((own[:-1], chunks[1]))
    first = join(early)
    pairs = [list(range(c, c + CORES)) for c in range(0, chips * CORES, CORES)]
    both = lax.all_gather(first, "blk", axis=0, axis_index_groups=pairs)
    first, last, both, chunks = lax.optimization_barrier((first, own[-1], both, chunks))
    chunks = [chunks[0]] + [chunks[1 + far.index(m)] for m in range(1, chips)]
    there = swap(last, "blk", 1)
    scores = pair_scores(0, first, last, chunks, ())
    scores = pair_scores(1, both, there, chunks, (mask, *scores))
    total = scores[0]
    for m in [k ^ (k >> 1) for k in range(1, chips)]:
        total = total + swap(scores[m], "blk", CORES * m)
    return total


def solution(mesh):
    in_specs = (
        P(("seq", "blk"), None),
        P(("seq", "blk"), None),
        P(),
        P(),
        P("blk", "seq", None),
        P("blk", "seq", None),
        P("blk", "seq", None),
        P("blk", "seq", None),
        P("blk", "seq", None),
    )
    out_specs = P(None, ("seq", "blk"))
    return jax.shard_map(
        on_device, mesh=mesh, in_specs=in_specs, out_specs=out_specs, check_vma=False
    )
```

```python
import functools

import jax
import jax.numpy as jnp
from jax import lax
from jax.experimental import pallas as pl
from jax.experimental.pallas import tpu as pltpu
from jax.sharding import PartitionSpec as P

BLOCK = 256
SEQ_LEN = 1024
QUERIES = 8
QTOK = 32
DAMPING = 0.1
CORES = 2
WIDTH = 4
PACK_VMEM = 16 * 1024 * 1024
VMEM_BYTES = 24 * 1024 * 1024

VMEM = pl.BlockSpec(memory_space=pltpu.VMEM)
HBM = pl.BlockSpec(memory_space=pltpu.HBM)
TT = (((0,), (1,)), ((), ()))
TN = (((0,), (0,)), ((), ()))


def swap(array, axis, bits):
    return lax.ppermute(array, axis, [(i, i ^ bits) for i in range(lax.axis_size(axis))])


def valid_mask(lengths, sequences, start, shape):
    position = start + lax.broadcasted_iota(jnp.int32, shape, 1)
    low = start // SEQ_LEN
    valid = jnp.zeros(shape, jnp.float32)
    for s in range((shape[1] + SEQ_LEN - 2) // SEQ_LEN + 1):
        sequence = jnp.minimum(low + s, sequences - 1)
        offset = position - sequence * SEQ_LEN
        valid = jnp.where((offset >= 0) & (offset < lengths[sequence]), 1.0, valid)
    return valid


def copy_blocks(table, distances, acts_ref, grads_ref, chunks, sem):
    me = lax.axis_index("blk")
    copies = []
    for m, chunk in zip(distances, chunks):
        for core in range(CORES):
            owner = me ^ (CORES * m + core)
            for half, (source, row) in enumerate(((acts_ref, 1), (grads_ref, 0))):
                start = pl.multiple_of(table[row, owner] * BLOCK, BLOCK)
                copy = pltpu.make_async_copy(
                    source.at[:, pl.ds(start, BLOCK)],
                    chunk.at[core, :, pl.ds(half * BLOCK, BLOCK)],
                    sem.at[len(copies)],
                )
                copy.start()
                copies.append(copy)
    return copies


def blocks_kernel(distances, table_ref, lengths_ref, acts_ref, grads_ref, mask_ref, *refs):
    chunks, (table, lengths, sem) = refs[:-3], refs[-3:]
    count = 2 * CORES * len(distances)
    scalars = [
        pltpu.make_async_copy(table_ref, table, sem.at[count]),
        pltpu.make_async_copy(lengths_ref, lengths, sem.at[count + 1]),
    ]
    for copy in scalars:
        copy.start()
    scalars[0].wait()
    copies = copy_blocks(table, distances, acts_ref, grads_ref, chunks, sem)
    scalars[1].wait()
    me = lax.axis_index("blk")
    group = lax.axis_index("seq") * lax.axis_size("blk")
    chips, _, tokens = mask_ref.shape
    for m in range(chips):
        start = (group + (me ^ (CORES * m))) * tokens
        mask_ref[m] = valid_mask(lengths, lengths_ref.shape[0], start, mask_ref.shape[1:])
    for copy in copies:
        copy.wait()


def take_blocks(distances, table, lengths, acts, grads):
    tokens, chips = acts.shape[0], table.shape[1] // CORES
    operands = [
        pltpu.with_memory_space_constraint(a, pltpu.HBM) for a in (table, lengths, acts, grads)
    ]
    return pl.pallas_call(
        functools.partial(blocks_kernel, distances),
        out_shape=(pltpu.VMEM((chips, QUERIES, tokens), jnp.float32),)
        + (pltpu.VMEM((CORES, tokens, 2 * BLOCK), jnp.bfloat16),) * len(distances),
        in_specs=[HBM] * 4,
        out_specs=(VMEM,) * (1 + len(distances)),
        scratch_shapes=[
            pltpu.SMEM(table.shape, jnp.int32),
            pltpu.SMEM(lengths.shape, jnp.int32),
            pltpu.SemaphoreType.DMA((2 * CORES * len(distances) + 2,)),
        ],
        compiler_params=pltpu.CompilerParams(vmem_limit_bytes=VMEM_BYTES),
        name="take_blocks",
    )(*operands)


def pack_kernel(distances, table_ref, acts_ref, grads_ref, *refs):
    shards, packed_ref = refs[:5], refs[5]
    chunks, (raw_eigen, table, sem) = refs[6:-3], refs[-3:]
    rows = raw_eigen.shape[0]
    fetch = pltpu.make_async_copy(table_ref, table, sem.at[0])
    fetch.start()
    weights = []
    for part, shard in enumerate(shards):
        target = raw_eigen if part == 4 else packed_ref.at[pl.ds(part * rows, rows), :]
        weights.append(pltpu.make_async_copy(shard.at[0], target, sem.at[1 + part]))
    for copy in weights:
        copy.start()
    fetch.wait()
    copies = copy_blocks(table, distances, acts_ref, grads_ref, chunks, sem.at[pl.ds(6, 2 * CORES)])
    for copy in weights:
        copy.wait()
    packed_ref[4 * rows :, :] = raw_eigen[...].astype(jnp.bfloat16)
    for copy in copies:
        copy.wait()


def pack(distances, table, acts, grads, *shards):
    tokens, rows = acts.shape[0], shards[0].shape[1]
    chunk = pltpu.VMEM((CORES, tokens, 2 * BLOCK), jnp.bfloat16)
    packed = pltpu.VMEM((5 * rows, BLOCK), jnp.bfloat16)
    operands = [pltpu.with_memory_space_constraint(a, pltpu.HBM) for a in (table, acts, grads, *shards)]
    return pl.pallas_call(
        functools.partial(pack_kernel, distances),
        out_shape=(packed,) + (chunk,) * len(distances),
        in_specs=[HBM] * len(operands),
        out_specs=(VMEM,) * (1 + len(distances)),
        scratch_shapes=[
            pltpu.VMEM((rows, BLOCK), jnp.float32),
            pltpu.SMEM(table.shape, jnp.int32),
            pltpu.SemaphoreType.DMA((6 + 2 * CORES * len(distances),)),
        ],
        compiler_params=pltpu.CompilerParams(vmem_limit_bytes=PACK_VMEM),
        name="pack",
    )(*operands)


def join_kernel(*refs):
    pieces, out = refs[:-1], refs[-1]
    rows = pieces[0].shape[0]
    for m, piece in enumerate(pieces):
        out[m * rows : (m + 1) * rows, :] = piece[...]


def join(pieces):
    rows = pieces[0].shape[0]
    return pl.pallas_call(
        join_kernel,
        out_shape=jax.ShapeDtypeStruct((len(pieces) * rows, BLOCK), jnp.bfloat16),
        in_specs=[VMEM] * len(pieces),
        out_specs=VMEM,
        compiler_params=pltpu.CompilerParams(vmem_limit_bytes=VMEM_BYTES),
        name="join",
    )(*pieces)


def pair_kernel(core, rows, chips, first_ref, last_ref, *refs):
    chunks, before = refs[:chips], refs[chips : -chips - 2]
    outs, full, precond = refs[-chips - 2 : -2], refs[-2], refs[-1]
    me = lax.axis_index("seq")
    if core:
        first_ref = first_ref.at[1 - lax.rem(lax.axis_index("blk"), CORES)]
    m = 0
    for pieces in (first_ref, last_ref):
        for first in range(0, pieces.shape[0], 5 * rows):
            place = pl.ds(pl.multiple_of((me ^ m) * rows, rows), rows)
            for part in range(5):
                start = first + part * rows
                full[part, place, :] = pieces[start : start + rows, :]
            m += 1
    basis_act, basis_grad = full[0], full[1]
    qrot_acts = jnp.dot(full[2], basis_act, preferred_element_type=jnp.float32).astype(jnp.bfloat16)
    qrot_grads = jnp.dot(full[3], basis_grad, preferred_element_type=jnp.float32).astype(jnp.bfloat16)
    scale = 1.0 / (QTOK * (full[4].astype(jnp.float32) + DAMPING))
    tokens = chunks[0].shape[1]
    for m in range(0, chips, WIDTH):
        some = chunks[m : m + WIDTH]
        acts = jnp.concatenate([c[core, :, :BLOCK] for c in some], axis=0)
        grads = jnp.concatenate([c[core, :, BLOCK:] for c in some], axis=0)
        rot_acts = lax.dot_general(
            basis_act, acts, TT, preferred_element_type=jnp.float32
        ).astype(jnp.bfloat16)
        rot_grads = lax.dot_general(basis_grad, grads, TT, preferred_element_type=jnp.float32)
        if m == 0:
            for q in range(QUERIES):
                rows_q = slice(q * QTOK, (q + 1) * QTOK)
                outer = lax.dot_general(
                    qrot_grads[rows_q], qrot_acts[rows_q], TN, preferred_element_type=jnp.float32
                )
                precond[q] = (outer * scale).astype(jnp.bfloat16)
        sums = []
        for q in range(QUERIES):
            mixed = jnp.dot(precond[q], rot_acts, preferred_element_type=jnp.float32)
            sums.append(jnp.sum(mixed * rot_grads, axis=0, keepdims=True))
        scores = jnp.concatenate(sums, axis=0)
        for s in range(len(some)):
            part = scores[:, s * tokens : (s + 1) * tokens]
            if core:
                part = jnp.where(before[0][m + s] > 0, part + before[1 + m + s][...], 0.0)
            outs[m + s][...] = part


def pair_scores(core, first, last, chunks, before):
    chips, tokens = len(chunks), chunks[0].shape[1]
    rows = BLOCK // lax.axis_size("seq")
    operands = (first, last, *chunks, *before)
    return pl.pallas_call(
        functools.partial(pair_kernel, core, rows, chips),
        out_shape=(jax.ShapeDtypeStruct((QUERIES, tokens), jnp.float32),) * chips,
        in_specs=[VMEM] * len(operands),
        out_specs=(VMEM,) * chips,
        scratch_shapes=[
            pltpu.VMEM((5, BLOCK, BLOCK), jnp.bfloat16),
            pltpu.VMEM((QUERIES, BLOCK, BLOCK), jnp.bfloat16),
        ],
        compiler_params=pltpu.CompilerParams(vmem_limit_bytes=VMEM_BYTES),
        cost_estimate=pl.CostEstimate(
            flops=2 * chips * tokens * BLOCK * BLOCK * (QUERIES + 2),
            bytes_accessed=2 * BLOCK * (chips * tokens * 2 + BLOCK * (QUERIES + 2)),
            transcendentals=0,
        ),
        name="pair_scores",
    )(*operands)


def on_device(
    train_acts,
    train_grads,
    block_table,
    seq_lengths,
    query_acts,
    query_grads,
    basis_acts,
    basis_grads,
    eigenvalues,
):
    groups, chips = lax.axis_size("seq"), lax.axis_size("blk") // CORES
    far = sorted(range(1, chips), key=lambda m: (-m.bit_count(), -m))
    packed, *ahead = pack(
        far[:1],
        block_table.T,
        train_acts,
        train_grads,
        basis_acts,
        basis_grads,
        query_acts,
        query_grads,
        eigenvalues,
    )
    own = [packed]
    for m in range(1, groups):
        own.append(swap(own[m & (m - 1)], "seq", m & -m))
    others = far[1:] + [0]
    mask, *later = take_blocks(others, block_table.T, seq_lengths, train_acts, train_grads)
    chunks = dict(zip(far[:1] + others, ahead + later))
    chunks = [chunks[0]] + [swap(chunks[m], "blk", CORES * m) for m in far]
    early, chunks[1] = lax.optimization_barrier((own[:-1], chunks[1]))
    first = join(early)
    pairs = [list(range(c, c + CORES)) for c in range(0, chips * CORES, CORES)]
    both = lax.all_gather(first, "blk", axis=0, axis_index_groups=pairs)
    first, last, both, chunks = lax.optimization_barrier((first, own[-1], both, chunks))
    chunks = [chunks[0]] + [chunks[1 + far.index(m)] for m in range(1, chips)]
    there = swap(last, "blk", 1)
    scores = pair_scores(0, first, last, chunks, ())
    scores = pair_scores(1, both, there, chunks, (mask, *scores))
    total = scores[0]
    for m in [k ^ (k >> 1) for k in range(1, chips)]:
        total = total + swap(scores[m], "blk", CORES * m)
    return total


def solution(mesh):
    in_specs = (
        P(("seq", "blk"), None),
        P(("seq", "blk"), None),
        P(),
        P(),
        P("blk", "seq", None),
        P("blk", "seq", None),
        P("blk", "seq", None),
        P("blk", "seq", None),
        P("blk", "seq", None),
    )
    out_specs = P(None, ("seq", "blk"))
    return jax.shard_map(
        on_device, mesh=mesh, in_specs=in_specs, out_specs=out_specs, check_vma=False
    )
```

```python
import functools

import jax
import jax.numpy as jnp
from jax import lax
from jax.experimental import pallas as pl
from jax.experimental.pallas import tpu as pltpu
from jax.sharding import PartitionSpec as P

BLOCK = 256
SEQ_LEN = 1024
QUERIES = 8
QTOK = 32
DAMPING = 0.1
CORES = 2
WIDTH = 4
PACK_VMEM = 16 * 1024 * 1024
VMEM_BYTES = 24 * 1024 * 1024

VMEM = pl.BlockSpec(memory_space=pltpu.VMEM)
HBM = pl.BlockSpec(memory_space=pltpu.HBM)
TT = (((0,), (1,)), ((), ()))
TN = (((0,), (0,)), ((), ()))


def swap(array, axis, bits):
    return lax.ppermute(array, axis, [(i, i ^ bits) for i in range(lax.axis_size(axis))])


def valid_mask(lengths, sequences, start, shape):
    position = start + lax.broadcasted_iota(jnp.int32, shape, 1)
    low = start // SEQ_LEN
    valid = jnp.zeros(shape, jnp.float32)
    for s in range((shape[1] + SEQ_LEN - 2) // SEQ_LEN + 1):
        sequence = jnp.minimum(low + s, sequences - 1)
        offset = position - sequence * SEQ_LEN
        valid = jnp.where((offset >= 0) & (offset < lengths[sequence]), 1.0, valid)
    return valid


def copy_blocks(table, distances, acts_ref, grads_ref, chunks, sem):
    me = lax.axis_index("blk")
    copies = []
    for m, chunk in zip(distances, chunks):
        for core in range(CORES):
            owner = me ^ (CORES * m + core)
            for half, (source, row) in enumerate(((acts_ref, 1), (grads_ref, 0))):
                start = pl.multiple_of(table[row, owner] * BLOCK, BLOCK)
                copy = pltpu.make_async_copy(
                    source.at[:, pl.ds(start, BLOCK)],
                    chunk.at[core, :, pl.ds(half * BLOCK, BLOCK)],
                    sem.at[len(copies)],
                )
                copy.start()
                copies.append(copy)
    return copies


def blocks_kernel(distances, table_ref, lengths_ref, acts_ref, grads_ref, mask_ref, *refs):
    chunks, (table, lengths, sem) = refs[:-3], refs[-3:]
    count = 2 * CORES * len(distances)
    scalars = [
        pltpu.make_async_copy(table_ref, table, sem.at[count]),
        pltpu.make_async_copy(lengths_ref, lengths, sem.at[count + 1]),
    ]
    for copy in scalars:
        copy.start()
    scalars[0].wait()
    copies = copy_blocks(table, distances, acts_ref, grads_ref, chunks, sem)
    scalars[1].wait()
    me = lax.axis_index("blk")
    group = lax.axis_index("seq") * lax.axis_size("blk")
    chips, _, tokens = mask_ref.shape
    for m in range(chips):
        start = (group + (me ^ (CORES * m))) * tokens
        mask_ref[m] = valid_mask(lengths, lengths_ref.shape[0], start, mask_ref.shape[1:])
    for copy in copies:
        copy.wait()


def take_blocks(distances, table, lengths, acts, grads):
    tokens, chips = acts.shape[0], table.shape[1] // CORES
    operands = [
        pltpu.with_memory_space_constraint(a, pltpu.HBM) for a in (table, lengths, acts, grads)
    ]
    return pl.pallas_call(
        functools.partial(blocks_kernel, distances),
        out_shape=(pltpu.VMEM((chips, QUERIES, tokens), jnp.float32),)
        + (pltpu.VMEM((CORES, tokens, 2 * BLOCK), jnp.bfloat16),) * len(distances),
        in_specs=[HBM] * 4,
        out_specs=(VMEM,) * (1 + len(distances)),
        scratch_shapes=[
            pltpu.SMEM(table.shape, jnp.int32),
            pltpu.SMEM(lengths.shape, jnp.int32),
            pltpu.SemaphoreType.DMA((2 * CORES * len(distances) + 2,)),
        ],
        compiler_params=pltpu.CompilerParams(vmem_limit_bytes=VMEM_BYTES),
        name="take_blocks",
    )(*operands)


def pack_kernel(distances, table_ref, acts_ref, grads_ref, *refs):
    shards, packed_ref = refs[:5], refs[5]
    chunks, (raw_eigen, table, sem) = refs[6:-3], refs[-3:]
    rows = raw_eigen.shape[0]
    fetch = pltpu.make_async_copy(table_ref, table, sem.at[0])
    fetch.start()
    weights = []
    for part, shard in enumerate(shards):
        target = raw_eigen if part == 4 else packed_ref.at[pl.ds(part * rows, rows), :]
        weights.append(pltpu.make_async_copy(shard.at[0], target, sem.at[1 + part]))
    for copy in weights:
        copy.start()
    fetch.wait()
    copies = copy_blocks(table, distances, acts_ref, grads_ref, chunks, sem.at[pl.ds(6, 2 * CORES)])
    for copy in weights:
        copy.wait()
    packed_ref[4 * rows :, :] = raw_eigen[...].astype(jnp.bfloat16)
    for copy in copies:
        copy.wait()


def pack(distances, table, acts, grads, *shards):
    tokens, rows = acts.shape[0], shards[0].shape[1]
    chunk = pltpu.VMEM((CORES, tokens, 2 * BLOCK), jnp.bfloat16)
    packed = pltpu.VMEM((5 * rows, BLOCK), jnp.bfloat16)
    operands = [pltpu.with_memory_space_constraint(a, pltpu.HBM) for a in (table, acts, grads, *shards)]
    return pl.pallas_call(
        functools.partial(pack_kernel, distances),
        out_shape=(packed,) + (chunk,) * len(distances),
        in_specs=[HBM] * len(operands),
        out_specs=(VMEM,) * (1 + len(distances)),
        scratch_shapes=[
            pltpu.VMEM((rows, BLOCK), jnp.float32),
            pltpu.SMEM(table.shape, jnp.int32),
            pltpu.SemaphoreType.DMA((6 + 2 * CORES * len(distances),)),
        ],
        compiler_params=pltpu.CompilerParams(vmem_limit_bytes=PACK_VMEM),
        name="pack",
    )(*operands)


def pair_kernel(core, rows, chips, first_ref, last_ref, *refs):
    chunks, before = refs[:chips], refs[chips : -chips - 2]
    outs, full, precond = refs[-chips - 2 : -2], refs[-2], refs[-1]
    me = lax.axis_index("seq")
    if core:
        first_ref = first_ref.at[1 - lax.rem(lax.axis_index("blk"), CORES)]
    m = 0
    for pieces in (first_ref, last_ref):
        for first in range(0, pieces.shape[0], 5 * rows):
            place = pl.ds(pl.multiple_of((me ^ m) * rows, rows), rows)
            for part in range(5):
                start = first + part * rows
                full[part, place, :] = pieces[start : start + rows, :]
            m += 1
    basis_act, basis_grad = full[0], full[1]
    qrot_acts = jnp.dot(full[2], basis_act, preferred_element_type=jnp.float32).astype(jnp.bfloat16)
    qrot_grads = jnp.dot(full[3], basis_grad, preferred_element_type=jnp.float32).astype(jnp.bfloat16)
    scale = 1.0 / (QTOK * (full[4].astype(jnp.float32) + DAMPING))
    tokens = chunks[0].shape[1]
    for m in range(0, chips, WIDTH):
        some = chunks[m : m + WIDTH]
        acts = jnp.concatenate([c[core, :, :BLOCK] for c in some], axis=0)
        grads = jnp.concatenate([c[core, :, BLOCK:] for c in some], axis=0)
        rot_acts = lax.dot_general(
            basis_act, acts, TT, preferred_element_type=jnp.float32
        ).astype(jnp.bfloat16)
        rot_grads = lax.dot_general(basis_grad, grads, TT, preferred_element_type=jnp.float32)
        if m == 0:
            for q in range(QUERIES):
                rows_q = slice(q * QTOK, (q + 1) * QTOK)
                outer = lax.dot_general(
                    qrot_grads[rows_q], qrot_acts[rows_q], TN, preferred_element_type=jnp.float32
                )
                precond[q] = (outer * scale).astype(jnp.bfloat16)
        sums = []
        for q in range(QUERIES):
            mixed = jnp.dot(precond[q], rot_acts, preferred_element_type=jnp.float32)
            sums.append(jnp.sum(mixed * rot_grads, axis=0, keepdims=True))
        scores = jnp.concatenate(sums, axis=0)
        for s in range(len(some)):
            part = scores[:, s * tokens : (s + 1) * tokens]
            if core:
                part = jnp.where(before[0][m + s] > 0, part + before[1 + m + s][...], 0.0)
            outs[m + s][...] = part


def pair_scores(core, first, last, chunks, before):
    chips, tokens = len(chunks), chunks[0].shape[1]
    rows = BLOCK // lax.axis_size("seq")
    operands = (first, last, *chunks, *before)
    return pl.pallas_call(
        functools.partial(pair_kernel, core, rows, chips),
        out_shape=(jax.ShapeDtypeStruct((QUERIES, tokens), jnp.float32),) * chips,
        in_specs=[VMEM] * len(operands),
        out_specs=(VMEM,) * chips,
        scratch_shapes=[
            pltpu.VMEM((5, BLOCK, BLOCK), jnp.bfloat16),
            pltpu.VMEM((QUERIES, BLOCK, BLOCK), jnp.bfloat16),
        ],
        compiler_params=pltpu.CompilerParams(vmem_limit_bytes=VMEM_BYTES),
        cost_estimate=pl.CostEstimate(
            flops=2 * chips * tokens * BLOCK * BLOCK * (QUERIES + 2),
            bytes_accessed=2 * BLOCK * (chips * tokens * 2 + BLOCK * (QUERIES + 2)),
            transcendentals=0,
        ),
        name="pair_scores",
    )(*operands)


def on_device(
    train_acts,
    train_grads,
    block_table,
    seq_lengths,
    query_acts,
    query_grads,
    basis_acts,
    basis_grads,
    eigenvalues,
):
    groups, chips = lax.axis_size("seq"), lax.axis_size("blk") // CORES
    far = sorted(range(1, chips), key=lambda m: (-m.bit_count(), -m))
    packed, *ahead = pack(
        far[:1],
        block_table.T,
        train_acts,
        train_grads,
        basis_acts,
        basis_grads,
        query_acts,
        query_grads,
        eigenvalues,
    )
    own = [packed]
    for m in range(1, groups):
        own.append(swap(own[m & (m - 1)], "seq", m & -m))
    others = far[1:] + [0]
    mask, *later = take_blocks(others, block_table.T, seq_lengths, train_acts, train_grads)
    chunks = dict(zip(far[:1] + others, ahead + later))
    chunks = [chunks[0]] + [swap(chunks[m], "blk", CORES * m) for m in far]
    early, chunks[1] = lax.optimization_barrier((own[:-1], chunks[1]))
    first = jnp.concatenate(early, axis=0)
    pairs = [list(range(c, c + CORES)) for c in range(0, chips * CORES, CORES)]
    both = lax.all_gather(first, "blk", axis=0, axis_index_groups=pairs)
    first, last, both, chunks = lax.optimization_barrier((first, own[-1], both, chunks))
    chunks = [chunks[0]] + [chunks[1 + far.index(m)] for m in range(1, chips)]
    there = swap(last, "blk", 1)
    scores = pair_scores(0, first, last, chunks, ())
    scores = pair_scores(1, both, there, chunks, (mask, *scores))
    total = scores[0]
    for m in [k ^ (k >> 1) for k in range(1, chips)]:
        total = total + swap(scores[m], "blk", CORES * m)
    return total


def solution(mesh):
    in_specs = (
        P(("seq", "blk"), None),
        P(("seq", "blk"), None),
        P(),
        P(),
        P("blk", "seq", None),
        P("blk", "seq", None),
        P("blk", "seq", None),
        P("blk", "seq", None),
        P("blk", "seq", None),
    )
    out_specs = P(None, ("seq", "blk"))
    return jax.shard_map(
        on_device, mesh=mesh, in_specs=in_specs, out_specs=out_specs, check_vma=False
    )
```

```python
import functools

import jax
import jax.numpy as jnp
from jax import lax
from jax.experimental import pallas as pl
from jax.experimental.pallas import tpu as pltpu
from jax.sharding import PartitionSpec as P

BLOCK = 256
SEQ_LEN = 1024
QUERIES = 8
QTOK = 32
DAMPING = 0.1
CORES = 2
WIDTH = 4
PACK_VMEM = 16 * 1024 * 1024
VMEM_BYTES = 24 * 1024 * 1024

VMEM = pl.BlockSpec(memory_space=pltpu.VMEM)
HBM = pl.BlockSpec(memory_space=pltpu.HBM)
TT = (((0,), (1,)), ((), ()))
TN = (((0,), (0,)), ((), ()))


def swap(array, axis, bits):
    return lax.ppermute(array, axis, [(i, i ^ bits) for i in range(lax.axis_size(axis))])


def valid_mask(lengths, sequences, start, shape):
    position = start + lax.broadcasted_iota(jnp.int32, shape, 1)
    low = start // SEQ_LEN
    valid = jnp.zeros(shape, jnp.float32)
    for s in range((shape[1] + SEQ_LEN - 2) // SEQ_LEN + 1):
        sequence = jnp.minimum(low + s, sequences - 1)
        offset = position - sequence * SEQ_LEN
        valid = jnp.where((offset >= 0) & (offset < lengths[sequence]), 1.0, valid)
    return valid


def copy_blocks(table, distances, acts_ref, grads_ref, chunks, sem):
    me = lax.axis_index("blk")
    copies = []
    for m, chunk in zip(distances, chunks):
        for core in range(CORES):
            owner = me ^ (CORES * m + core)
            for half, (source, row) in enumerate(((acts_ref, 1), (grads_ref, 0))):
                start = pl.multiple_of(table[row, owner] * BLOCK, BLOCK)
                copy = pltpu.make_async_copy(
                    source.at[:, pl.ds(start, BLOCK)],
                    chunk.at[core, :, pl.ds(half * BLOCK, BLOCK)],
                    sem.at[len(copies)],
                )
                copy.start()
                copies.append(copy)
    return copies


def blocks_kernel(distances, table_ref, lengths_ref, acts_ref, grads_ref, mask_ref, *refs):
    chunks, (table, lengths, sem) = refs[:-3], refs[-3:]
    count = 2 * CORES * len(distances)
    scalars = [
        pltpu.make_async_copy(table_ref, table, sem.at[count]),
        pltpu.make_async_copy(lengths_ref, lengths, sem.at[count + 1]),
    ]
    for copy in scalars:
        copy.start()
    scalars[0].wait()
    copies = copy_blocks(table, distances, acts_ref, grads_ref, chunks, sem)
    scalars[1].wait()
    me = lax.axis_index("blk")
    group = lax.axis_index("seq") * lax.axis_size("blk")
    chips, _, tokens = mask_ref.shape
    for m in range(chips):
        start = (group + (me ^ (CORES * m))) * tokens
        mask_ref[m] = valid_mask(lengths, lengths_ref.shape[0], start, mask_ref.shape[1:])
    for copy in copies:
        copy.wait()


def take_blocks(distances, table, lengths, acts, grads):
    tokens, chips = acts.shape[0], table.shape[1] // CORES
    operands = [
        pltpu.with_memory_space_constraint(a, pltpu.HBM) for a in (table, lengths, acts, grads)
    ]
    return pl.pallas_call(
        functools.partial(blocks_kernel, distances),
        out_shape=(pltpu.VMEM((chips, QUERIES, tokens), jnp.float32),)
        + (pltpu.VMEM((CORES, tokens, 2 * BLOCK), jnp.bfloat16),) * len(distances),
        in_specs=[HBM] * 4,
        out_specs=(VMEM,) * (1 + len(distances)),
        scratch_shapes=[
            pltpu.SMEM(table.shape, jnp.int32),
            pltpu.SMEM(lengths.shape, jnp.int32),
            pltpu.SemaphoreType.DMA((2 * CORES * len(distances) + 2,)),
        ],
        compiler_params=pltpu.CompilerParams(vmem_limit_bytes=VMEM_BYTES),
        name="take_blocks",
    )(*operands)


def pack_kernel(distances, table_ref, acts_ref, grads_ref, *refs):
    shards, packed_ref = refs[:5], refs[5]
    chunks, (raw_eigen, table, sem) = refs[6:-3], refs[-3:]
    rows = raw_eigen.shape[0]
    fetch = pltpu.make_async_copy(table_ref, table, sem.at[0])
    fetch.start()
    weights = []
    for part, shard in enumerate(shards):
        target = raw_eigen if part == 4 else packed_ref.at[pl.ds(part * rows, rows), :]
        weights.append(pltpu.make_async_copy(shard.at[0], target, sem.at[1 + part]))
    for copy in weights:
        copy.start()
    fetch.wait()
    copies = copy_blocks(table, distances, acts_ref, grads_ref, chunks, sem.at[pl.ds(6, 2 * CORES)])
    for copy in weights:
        copy.wait()
    packed_ref[4 * rows :, :] = raw_eigen[...].astype(jnp.bfloat16)
    for copy in copies:
        copy.wait()


def pack(distances, table, acts, grads, *shards):
    tokens, rows = acts.shape[0], shards[0].shape[1]
    chunk = pltpu.VMEM((CORES, tokens, 2 * BLOCK), jnp.bfloat16)
    packed = pltpu.VMEM((5 * rows, BLOCK), jnp.bfloat16)
    operands = [pltpu.with_memory_space_constraint(a, pltpu.HBM) for a in (table, acts, grads, *shards)]
    return pl.pallas_call(
        functools.partial(pack_kernel, distances),
        out_shape=(packed,) + (chunk,) * len(distances),
        in_specs=[HBM] * len(operands),
        out_specs=(VMEM,) * (1 + len(distances)),
        scratch_shapes=[
            pltpu.VMEM((rows, BLOCK), jnp.float32),
            pltpu.SMEM(table.shape, jnp.int32),
            pltpu.SemaphoreType.DMA((6 + 2 * CORES * len(distances),)),
        ],
        compiler_params=pltpu.CompilerParams(vmem_limit_bytes=PACK_VMEM),
        name="pack",
    )(*operands)


def join_kernel(*refs):
    pieces, out = refs[:-1], refs[-1]
    rows = pieces[0].shape[0]
    for m, piece in enumerate(pieces):
        out[m * rows : (m + 1) * rows, :] = piece[...]


def join(pieces):
    rows = pieces[0].shape[0]
    return pl.pallas_call(
        join_kernel,
        out_shape=jax.ShapeDtypeStruct((len(pieces) * rows, BLOCK), jnp.bfloat16),
        in_specs=[VMEM] * len(pieces),
        out_specs=VMEM,
        compiler_params=pltpu.CompilerParams(vmem_limit_bytes=VMEM_BYTES),
        name="join",
    )(*pieces)


def pair_kernel(core, rows, chips, first_ref, last_ref, *refs):
    chunks, before = refs[:chips], refs[chips : -chips - 2]
    outs, full, precond = refs[-chips - 2 : -2], refs[-2], refs[-1]
    me = lax.axis_index("seq")
    if core:
        first_ref = first_ref.at[1 - lax.rem(lax.axis_index("blk"), CORES)]
    m = 0
    for pieces in (first_ref, last_ref):
        for first in range(0, pieces.shape[0], 5 * rows):
            place = pl.ds(pl.multiple_of((me ^ m) * rows, rows), rows)
            for part in range(5):
                start = first + part * rows
                full[part, place, :] = pieces[start : start + rows, :]
            m += 1
    basis_act, basis_grad = full[0], full[1]
    qrot_acts = jnp.dot(full[2], basis_act, preferred_element_type=jnp.float32).astype(jnp.bfloat16)
    qrot_grads = jnp.dot(full[3], basis_grad, preferred_element_type=jnp.float32).astype(jnp.bfloat16)
    scale = 1.0 / (QTOK * (full[4].astype(jnp.float32) + DAMPING))
    tokens = chunks[0].shape[1]
    for m in range(0, chips, WIDTH):
        some = chunks[m : m + WIDTH]
        acts = jnp.concatenate([c[core, :, :BLOCK] for c in some], axis=0)
        grads = jnp.concatenate([c[core, :, BLOCK:] for c in some], axis=0)
        rot_acts = lax.dot_general(
            basis_act, acts, TT, preferred_element_type=jnp.float32
        ).astype(jnp.bfloat16)
        rot_grads = lax.dot_general(basis_grad, grads, TT, preferred_element_type=jnp.float32)
        if m == 0:
            for q in range(QUERIES):
                rows_q = slice(q * QTOK, (q + 1) * QTOK)
                outer = lax.dot_general(
                    qrot_grads[rows_q], qrot_acts[rows_q], TN, preferred_element_type=jnp.float32
                )
                precond[q] = (outer * scale).astype(jnp.bfloat16)
        sums = []
        for q in range(QUERIES):
            mixed = jnp.dot(precond[q], rot_acts, preferred_element_type=jnp.float32)
            sums.append(jnp.sum(mixed * rot_grads, axis=0, keepdims=True))
        scores = jnp.concatenate(sums, axis=0)
        for s in range(len(some)):
            part = scores[:, s * tokens : (s + 1) * tokens]
            if core:
                part = jnp.where(before[0][m + s] > 0, part + before[1 + m + s][...], 0.0)
            outs[m + s][...] = part


def pair_scores(core, first, last, chunks, before):
    chips, tokens = len(chunks), chunks[0].shape[1]
    rows = BLOCK // lax.axis_size("seq")
    operands = (first, last, *chunks, *before)
    return pl.pallas_call(
        functools.partial(pair_kernel, core, rows, chips),
        out_shape=(jax.ShapeDtypeStruct((QUERIES, tokens), jnp.float32),) * chips,
        in_specs=[VMEM] * len(operands),
        out_specs=(VMEM,) * chips,
        scratch_shapes=[
            pltpu.VMEM((5, BLOCK, BLOCK), jnp.bfloat16),
            pltpu.VMEM((QUERIES, BLOCK, BLOCK), jnp.bfloat16),
        ],
        compiler_params=pltpu.CompilerParams(vmem_limit_bytes=VMEM_BYTES),
        cost_estimate=pl.CostEstimate(
            flops=2 * chips * tokens * BLOCK * BLOCK * (QUERIES + 2),
            bytes_accessed=2 * BLOCK * (chips * tokens * 2 + BLOCK * (QUERIES + 2)),
            transcendentals=0,
        ),
        name="pair_scores",
    )(*operands)


def on_device(
    train_acts,
    train_grads,
    block_table,
    seq_lengths,
    query_acts,
    query_grads,
    basis_acts,
    basis_grads,
    eigenvalues,
):
    groups, chips = lax.axis_size("seq"), lax.axis_size("blk") // CORES
    far = sorted(range(1, chips), key=lambda m: (-m.bit_count(), -m))
    packed, *ahead = pack(
        far[:1],
        block_table.T,
        train_acts,
        train_grads,
        basis_acts,
        basis_grads,
        query_acts,
        query_grads,
        eigenvalues,
    )
    own = [packed]
    for m in range(1, groups):
        own.append(swap(own[m & (m - 1)], "seq", m & -m))
    others = far[1:] + [0]
    mask, *later = take_blocks(others, block_table.T, seq_lengths, train_acts, train_grads)
    chunks = dict(zip(far[:1] + others, ahead + later))
    chunks = [chunks[0]] + [swap(chunks[m], "blk", CORES * m) for m in far]
    early, chunks[1] = lax.optimization_barrier((own[:-1], chunks[1]))
    first = join(early)
    pairs = [list(range(c, c + CORES)) for c in range(0, chips * CORES, CORES)]
    both = lax.all_gather(first, "blk", axis=0, axis_index_groups=pairs)
    first, last, both, chunks = lax.optimization_barrier((first, own[-1], both, chunks))
    chunks = [chunks[0]] + [chunks[1 + far.index(m)] for m in range(1, chips)]
    there = swap(last, "blk", 1)
    scores = pair_scores(0, first, last, chunks, ())
    scores = pair_scores(1, both, there, chunks, (mask, *scores))
    total = scores[0]
    for m in sorted(range(1, chips), key=lambda m: (-m.bit_count(), m)):
        total = total + swap(scores[m], "blk", CORES * m)
    return total


def solution(mesh):
    in_specs = (
        P(("seq", "blk"), None),
        P(("seq", "blk"), None),
        P(),
        P(),
        P("blk", "seq", None),
        P("blk", "seq", None),
        P("blk", "seq", None),
        P("blk", "seq", None),
        P("blk", "seq", None),
    )
    out_specs = P(None, ("seq", "blk"))
    return jax.shard_map(
        on_device, mesh=mesh, in_specs=in_specs, out_specs=out_specs, check_vma=False
    )
```
